256 devices in a mesh: dp: 64 (over y, z, core), tensor: 4 (over x).
Axes of the slice: x: 4, y: 4, z: 8, core: 2. Of those that a mesh axis runs over, the one named last changes fastest.
Arguments:
- query_raw: bfloat16 [24576, 3072], P('dp', 'tensor'), may hold values from -8000 to 8000
- key_raw: bfloat16 [24576, 3072], P('dp', 'tensor'), may hold values from -8000 to 8000
- value_rows: bfloat16 [24576, 3072], P('dp', 'tensor'), may hold values from -24 to 24
- gain_query: float32 [3072], P('tensor'), may hold values from 0.1 to 1.9
- gain_key: float32 [3072], P('tensor'), may hold values from 0.1 to 1.9
- owner_id: int32 [24576], P('dp'), may hold values from 0 to 63, as said below
- utterance: int32 [24576], P('dp'), may hold values from 0 to 1, as said below
- cotangent: bfloat16 [49152, 3072], P('dp', 'tensor'), may hold values from -18 to 18
Outputs:
- attended: bfloat16 [49152, 3072], P('dp', 'tensor')
- grad_query: bfloat16 [24576, 3072], P('dp', 'tensor')
- grad_key: bfloat16 [24576, 3072], P('dp', 'tensor')
- grad_value: bfloat16 [24576, 3072], P('dp', 'tensor')
- gain_grad_query: float32 [3072], P('tensor')
- gain_grad_key: float32 [3072], P('tensor')
The draws below stay inside these ranges and needn't reach their ends.
Inputs may be any that keep to these rules, and one draw needn't show every extreme that they name: `owner_id`: rows 2j and 2j+1 always have the same owner and the same utterance number. Of the 384 rows of one device at most 12 have the same owner; in every draw some owner gets 12 rows from every device. Rows with the same owner and the same number form one utterance.
All inputs are finite; a program needn't handle non-finite values.
Results may differ from the reference program's by a relative error of at most 0.017.
The reference program's roundings to bfloat16 on the way count: a program that leaves them out, or rounds other values in their place, can miss the bound.
Values may be sent and summed in bfloat16 or wider, within the bound.
A program may use at most 128 MiB of HBM per device.

```python
import math
import jax
import jax.numpy as jnp
from jax import lax

HEADS = 24
HD = 128
UMAX = 2
TOK_DEV = 384
TOKENS = 24576
SLOT = 12
OWN_ROWS = 768
FEAT = 3072
N_DP = 64


def feature_scales(key, rise):
    key_spread = jax.random.fold_in(key, 11)
    spread = jax.random.uniform(key_spread, (FEAT,), jnp.float32, 0.0, 1.0)
    position = jnp.arange(FEAT, dtype=jnp.float32) / FEAT
    return jnp.exp(math.log(rise) * position + math.log(3.3) * spread)


def routing(key):
    key_full, key_order, key_split, key_shuffle, key_count, key_label = jax.random.split(key, 6)
    half_slot = SLOT // 2
    pair_count = TOK_DEV // 2
    group_count = N_DP // 2
    full_owner = jax.random.randint(key_full, (), 0, N_DP)
    targets = jnp.arange(N_DP, dtype=jnp.int32)
    ranking = jax.random.randint(key_order, (N_DP, N_DP), 1, 1 << 20) * N_DP + targets[None, :]
    ranking = jnp.where(targets[None, :] == full_owner, 0, ranking)
    order_rows = jnp.argsort(ranking, axis=1).astype(jnp.int32)
    first_share = jax.random.randint(key_split, (N_DP, group_count), 0, half_slot + 1)
    first_share = first_share.at[:, 0].set(half_slot)
    pair_index = jnp.arange(pair_count, dtype=jnp.int32)
    group_of = pair_index // half_slot
    within_group = pair_index % half_slot
    leading = jnp.take(order_rows, 2 * group_of, axis=1)
    trailing = jnp.take(order_rows, 2 * group_of + 1, axis=1)
    cut_point = jnp.take(first_share, group_of, axis=1)
    pair_owner = jnp.where(within_group[None, :] < cut_point, leading, trailing)
    shuffle_keys = jax.random.randint(key_shuffle, (N_DP, pair_count), 0, 1 << 20) * pair_count + pair_index[None, :]
    shuffle_order = jnp.argsort(shuffle_keys, axis=1)
    pair_owner = jnp.take_along_axis(pair_owner, shuffle_order, axis=1)
    owner_counts = jax.random.randint(key_count, (N_DP,), 1, UMAX + 1).at[full_owner].set(UMAX)
    picks = jax.random.randint(key_label, (N_DP, pair_count), 0, 1 << 20)
    pair_label = picks % jnp.take(owner_counts, pair_owner)
    owners = jnp.repeat(pair_owner.reshape(-1), 2).astype(jnp.int32)
    labels = jnp.repeat(pair_label.reshape(-1), 2).astype(jnp.int32)
    return (owners, labels)


def draw_query_raw(key, part):
    scales = feature_scales(key, 3.0)
    key = jax.random.fold_in(key, 1)
    drawn = jax.random.truncated_normal(key, -5.0, 5.0, (TOKENS, FEAT), jnp.float32) * scales[None, :]
    return drawn.astype(jnp.bfloat16)


def draw_key_raw(key, part):
    scales = feature_scales(key, 3.0)
    key = jax.random.fold_in(key, 2)
    drawn = jax.random.truncated_normal(key, -5.0, 5.0, (TOKENS, FEAT), jnp.float32) * scales[None, :]
    return drawn.astype(jnp.bfloat16)


def draw_owner_id(key, part):
    owners, labels = routing(key)
    return owners


def draw_utterance(key, part):
    owners, labels = routing(key)
    return labels


def steps_of(key, extent, pieces, low, high):
    loudness, own = 1.0, jax.random.fold_in(key, 6)
    for axis_at, parts in pieces:
        draws = jnp.exp(jax.random.uniform(jax.random.fold_in(own, axis_at), (parts,), jnp.float32, low / len(pieces), high / len(pieces)))
        loudness = loudness * jnp.repeat(draws, extent[axis_at] // parts).reshape([-1 if axis == axis_at else 1 for axis in range(len(extent))])
    return loudness


def normal_values(own_key, shape, deviation, bound, cuts=(), kind=jnp.bfloat16):
    entries = deviation * jax.random.normal(own_key, shape, jnp.float32)
    if cuts:
        entries = entries * steps_of(own_key, shape, cuts, -0.22, 0.18)
    return jnp.clip(entries, -bound, bound).astype(kind)


def setup_inputs(seed: int = 0) -> dict:
    seeds = jax.random.split(jax.random.key(seed), 9)
    return {
        "query_raw": draw_query_raw(jax.random.fold_in(seeds[8], 71), 0),
        "key_raw": draw_key_raw(jax.random.fold_in(seeds[8], 71), 0),
        "value_rows": normal_values(seeds[2], (TOKENS, FEAT), 4.0, 24.0, ((0, 64), (1, 4))),
        "gain_query": jnp.clip(1.0 + 0.18 * jax.random.normal(seeds[3], (FEAT,), jnp.float32), 0.1, 1.9),
        "gain_key": jnp.clip(1.0 + 0.18 * jax.random.normal(seeds[4], (FEAT,), jnp.float32), 0.1, 1.9),
        "owner_id": draw_owner_id(jax.random.fold_in(seeds[8], 71), 0),
        "utterance": draw_utterance(jax.random.fold_in(seeds[8], 71), 0),
        "cotangent": normal_values(seeds[7], (N_DP * OWN_ROWS, FEAT), 3.0, 18.0, ((0, 64), (1, 4))),
    }


EPSILON = 1e-06
MASKED = -1e+30

def owner_places(owner_id):
    owner_grid = owner_id.reshape(N_DP, TOK_DEV)
    targets = jnp.arange(N_DP, dtype=jnp.int32)
    one_hot = (owner_grid[:, :, None] == targets[None, None, :]).astype(jnp.int32)
    earlier = jnp.cumsum(one_hot, axis=1) - one_hot
    rank_within = lax.optimization_barrier(jnp.sum(earlier * one_hot, axis=2))
    source_ids = jnp.arange(N_DP, dtype=jnp.int32)[:, None]
    return (owner_grid * OWN_ROWS + source_ids * SLOT + rank_within).reshape(-1).astype(jnp.int32)

def unit_rows(raw_rows):
    values_f = raw_rows.astype(jnp.float32)
    inverse = lax.rsqrt(lax.optimization_barrier(jnp.mean(values_f * values_f, axis=1, keepdims=True)) + EPSILON)
    return (values_f * inverse, inverse)

def norm_grad(grad_n, unit, inverse, gain):
    scaled = gain[None, :] * grad_n.astype(jnp.float32)
    center = lax.optimization_barrier(jnp.mean(scaled * unit, axis=1, keepdims=True))
    return ((scaled - unit * center) * inverse).astype(jnp.bfloat16)

def owner_block(block):
    query_rows, key_rows, value_own, labels, cotangent = block
    factor = HD ** (-0.5)
    query_f = query_rows.reshape(OWN_ROWS, HEADS, HD).astype(jnp.float32)
    key_f = key_rows.reshape(OWN_ROWS, HEADS, HD).astype(jnp.float32)
    value_f = value_own.reshape(OWN_ROWS, HEADS, HD).astype(jnp.float32)
    scores = jnp.einsum('ihd,jhd->hij', query_f, key_f) * factor
    allowed = (labels[:, None] == labels[None, :])[None, :, :]
    scores = jnp.where(allowed, scores, MASKED)
    raised = jnp.exp(scores - lax.optimization_barrier(jnp.max(scores, axis=2, keepdims=True)))
    weights = (raised / lax.optimization_barrier(jnp.sum(raised, axis=2, keepdims=True))).astype(jnp.bfloat16)
    weights = lax.optimization_barrier(weights).astype(jnp.float32)
    attended = jnp.einsum('hij,jhd->ihd', weights, value_f).astype(jnp.bfloat16)
    attended_f = lax.optimization_barrier(attended).astype(jnp.float32)
    grad_f = cotangent.reshape(OWN_ROWS, HEADS, HD).astype(jnp.float32)
    delta = lax.optimization_barrier(jnp.sum(grad_f * attended_f, axis=2))
    grad_value = jnp.einsum('hij,ihd->jhd', weights, grad_f).astype(jnp.bfloat16)
    grad_weights = jnp.einsum('ihd,jhd->hij', grad_f, value_f)
    grad_scores = (weights * (grad_weights - jnp.transpose(delta)[:, :, None])).astype(jnp.bfloat16)
    grad_scores = lax.optimization_barrier(grad_scores).astype(jnp.float32)
    grad_query = (jnp.einsum('hij,jhd->ihd', grad_scores, key_f) * factor).astype(jnp.bfloat16)
    grad_key = (jnp.einsum('hij,ihd->jhd', grad_scores, query_f) * factor).astype(jnp.bfloat16)
    return (attended.reshape(OWN_ROWS, FEAT), grad_query.reshape(OWN_ROWS, FEAT), grad_key.reshape(OWN_ROWS, FEAT), grad_value.reshape(OWN_ROWS, FEAT))

def reference(query_raw, key_raw, value_rows, gain_query, gain_key, owner_id, utterance, cotangent):
    places = owner_places(owner_id)
    total_rows = N_DP * OWN_ROWS
    unit_query, inverse_query = unit_rows(query_raw)
    unit_key, inverse_key = unit_rows(key_raw)
    query_n = (gain_query[None, :] * unit_query).astype(jnp.bfloat16)
    key_n = (gain_key[None, :] * unit_key).astype(jnp.bfloat16)

    def spread(rows, filler):
        return jnp.full((total_rows,) + rows.shape[1:], filler, rows.dtype).at[places].set(rows)
    blocks = (spread(query_n, 0).reshape(N_DP, OWN_ROWS, FEAT), spread(key_n, 0).reshape(N_DP, OWN_ROWS, FEAT), spread(value_rows, 0).reshape(N_DP, OWN_ROWS, FEAT), spread(utterance, -1).reshape(N_DP, OWN_ROWS), cotangent.reshape(N_DP, OWN_ROWS, FEAT))
    attended, grad_query_own, grad_key_own, grad_value_own = lax.map(owner_block, blocks)
    attended = attended.reshape(total_rows, FEAT)
    grad_query_n = grad_query_own.reshape(total_rows, FEAT)[places]
    grad_key_n = grad_key_own.reshape(total_rows, FEAT)[places]
    grad_value = grad_value_own.reshape(total_rows, FEAT)[places]
    grad_query = norm_grad(grad_query_n, unit_query, inverse_query, gain_query)
    grad_key = norm_grad(grad_key_n, unit_key, inverse_key, gain_key)
    gain_grad_query = lax.optimization_barrier(jnp.sum(grad_query_n.astype(jnp.float32) * unit_query, axis=0))
    gain_grad_key = lax.optimization_barrier(jnp.sum(grad_key_n.astype(jnp.float32) * unit_key, axis=0))
    return (attended, grad_query, grad_key, grad_value, gain_grad_query, gain_grad_key)
```

```python
import functools
import math

import jax
import jax.numpy as jnp
from jax import lax
from jax.experimental import pallas as pl
from jax.experimental.pallas import tpu as pltpu
from jax.sharding import PartitionSpec as P

HD = 128
EPSILON = 1e-06
SLOT = 12
TILE = 16
HEADS = 6
GROUPS = 3
FAR = -(2.0**30)
F32 = jnp.float32
BF16 = jnp.bfloat16
MESH = pl.DeviceIdType.MESH
SHAPES = {64: (4, 8, 2), 16: (2, 4, 2), 8: (2, 2, 2)}


def mm(a, b):
    return lax.dot_general(a, b, (((1,), (0,)), ((), ())), preferred_element_type=F32)


def mm_nt(a, b):
    return lax.dot_general(a, b, (((1,), (1,)), ((), ())), preferred_element_type=F32)


def mm_tn(a, b):
    return lax.dot_general(a, b, (((0,), (0,)), ((), ())), preferred_element_type=F32)


def iota(shape, axis):
    return lax.broadcasted_iota(jnp.int32, shape, axis)


def ones_where(mask):
    return jnp.where(mask, 1.0, 0.0).astype(BF16)


def to_i32(x):
    return x.astype(jnp.int32)


def kernel(
    dp,
    tensors,
    tokens,
    query_ref,
    key_ref,
    value_ref,
    gain_query_ref,
    gain_key_ref,
    owner_ref,
    utterance_ref,
    cotangent_ref,
    attended_ref,
    grad_query_ref,
    grad_key_ref,
    grad_value_ref,
    gain_out_ref,
    pack_first,
    pack_second,
    pack_label,
    unpack_first,
    unpack_low,
    unpack_high_a,
    unpack_high_b,
    normed,
    inverse_query_ref,
    inverse_key_ref,
    send_value,
    recv_value,
    send_qk,
    recv_qk,
    back_qk,
    home_qk,
    back_value,
    home_value,
    value_own,
    grad_value_own,
    extend_query,
    extend_key,
    query_own,
    key_own,
    grad_query_own,
    key_sum,
    value_sum,
    grad_qn,
    grad_kn,
    stat_norm,
    stat_center,
    gain_near,
    gain_far,
    send_sems,
    recv_sems,
):
    size_y, size_z, size_c = SHAPES[dp]
    me = lax.axis_index("dp")
    my_x = lax.axis_index("tensor")
    my_c = me % size_c
    my_z = (me // size_c) % size_z
    my_y = me // (size_c * size_z)
    rows = dp * TILE
    own = dp * SLOT
    feat = HEADS * HD
    feat_total = feat * tensors
    blocks = dp // 16

    def peer_of(step):
        fast = step % size_z
        rest = step // size_z
        step_z = (fast % 2) * ((fast + 1) // 2) + (1 - fast % 2) * (size_z - fast // 2)
        to_y = (my_y + rest % size_y) % size_y
        to_z = (my_z + step_z) % size_z
        to_c = (my_c + rest // size_y) % size_c
        return (to_y * size_z + to_z) * size_c + to_c

    def scatter(source, target, index):
        own_copy = pltpu.make_async_copy(source.at[me], target.at[me], recv_sems.at[index])
        own_copy.start()

        def step_body(step, carry):
            peer = peer_of(step)
            pltpu.make_async_remote_copy(
                src_ref=source.at[peer],
                dst_ref=target.at[me],
                send_sem=send_sems.at[index],
                recv_sem=recv_sems.at[index],
                device_id={"dp": peer},
                device_id_type=MESH,
            ).start()
            return carry

        lax.fori_loop(1, dp, step_body, 0)

    def wait_recv(target, index):
        pltpu.make_async_copy(target, target, recv_sems.at[index]).wait()

    def wait_send(source, index, count):
        part = source.at[pl.ds(0, count)]
        pltpu.make_async_copy(part, part, send_sems.at[index]).wait()

    def share(buffer, slot, count, device_of, index):
        def step_body(step, carry):
            to = lax.rem(slot + step, count)
            pltpu.make_async_remote_copy(
                src_ref=buffer.at[slot],
                dst_ref=buffer.at[slot],
                send_sem=send_sems.at[index],
                recv_sem=recv_sems.at[index],
                device_id=device_of(to),
                device_id_type=MESH,
            ).start()
            return carry

        lax.fori_loop(1, count, step_body, 0)

    def share_wait(buffer, count, index):
        part = buffer.at[pl.ds(0, count - 1)]
        pltpu.make_async_copy(part, part, recv_sems.at[index]).wait()

    VALUE, QK, BACK_QK, BACK_VALUE, NORM, CENTER, NEAR, FARTHER = 0, 1, 4, 7, 8, 9, 10, 11

    owner_row = owner_ref[...]
    chosen = jnp.where(iota((dp, tokens), 0) == owner_row, 1.0, 0.0)
    upper = ones_where(iota((tokens, tokens), 0) < iota((tokens, tokens), 1))
    rank_row = jnp.sum(mm(chosen.astype(BF16), upper) * chosen, axis=0, keepdims=True)
    code_row_f = owner_row.astype(F32) * TILE + rank_row
    diagonal = iota((tokens, tokens), 0) == iota((tokens, tokens), 1)

    def as_column(row):
        return jnp.sum(jnp.where(diagonal, row, 0.0), axis=1, keepdims=True)

    rank_row = to_i32(rank_row)
    code_row = to_i32(code_row_f)
    none = -1

    def pack_block(block, carry):
        at = block * 256
        span = pl.ds(at, 256)
        row = iota((256, tokens), 0) + at
        pack_first[span, 0:tokens] = ones_where(row == code_row)
        pack_first[span, tokens : 2 * tokens] = ones_where(
            row == jnp.where(rank_row < 4, code_row + 12, none)
        )
        high = jnp.where(rank_row >= 4, code_row - 4, none)
        pack_second[span, 0:tokens] = ones_where(row == high)
        pack_second[span, tokens : 2 * tokens] = ones_where(
            row == jnp.where(rank_row >= 4, code_row + 4, none)
        )
        pack_label[span, :] = ones_where(row == jnp.where(rank_row < 8, code_row + 8, none))
        return carry

    lax.fori_loop(0, blocks, pack_block, 0)

    utterance_col = as_column(utterance_ref[...].astype(F32))
    lane = iota((tokens, HD), 1)
    label_low = ones_where(lane == to_i32(utterance_col))
    label_high = ones_where(lane == to_i32(utterance_col) + 64)

    def pack_value(block, carry):
        span = pl.ds(pl.multiple_of(block * 256, 256), 256)
        out = pl.ds(block * 16, 16)
        first = pack_first[span, :]
        second = pack_second[span, :]
        v = [value_ref[:, h * HD : (h + 1) * HD] for h in range(HEADS)]
        stack = lambda *parts: jnp.concatenate(parts, axis=0)

        def put(lo, part):
            width = part.shape[1]
            send_value[out, :, lo : lo + width] = part.astype(BF16).reshape(16, TILE, width)

        put(0, mm(first, stack(v[0], v[1])))
        put(128, mm(first, stack(v[2], v[3])))
        put(256, mm(second, stack(v[1], v[3])))
        put(384, mm(first, stack(v[4], v[5])))
        put(512, mm(second, stack(v[5], label_high)) + mm(pack_label[span, :], label_low))
        return carry

    lax.fori_loop(0, blocks, pack_value, 0)
    scatter(send_value, recv_value, VALUE)

    query_f = query_ref[...].astype(F32)
    key_f = key_ref[...].astype(F32)
    half = iota((tokens, HD), 1) < 64
    stat_norm[my_x] = jnp.where(
        half,
        jnp.sum(query_f * query_f, axis=1, keepdims=True),
        jnp.sum(key_f * key_f, axis=1, keepdims=True),
    )
    share(stat_norm, my_x, tensors, lambda to: {"tensor": to}, NORM)

    code_col = to_i32(as_column(code_row_f))
    rank_col = code_col % TILE
    column = iota((tokens, rows), 1)
    unpack_first[...] = ones_where(column == code_col)
    unpack_low[...] = ones_where(column == jnp.where(rank_col < 4, code_col + 12, none))
    unpack_high_a[...] = ones_where(column == jnp.where(rank_col >= 4, code_col - 4, none))
    unpack_high_b[...] = ones_where(column == jnp.where(rank_col >= 4, code_col + 4, none))

    share_wait(stat_norm, tensors, NORM)
    total = stat_norm[0]
    for x in range(1, tensors):
        total = total + stat_norm[x]
    inverse = lax.rsqrt(total / feat_total + EPSILON)
    inverse_query_ref[...] = jnp.broadcast_to(inverse[:, 0:1], (tokens, HD))
    inverse_key_ref[...] = jnp.broadcast_to(inverse[:, 64:65], (tokens, HD))
    for h in range(HEADS):
        cols = slice(h * HD, (h + 1) * HD)
        normed[0:tokens, cols] = (
            gain_query_ref[:, cols] * (query_ref[:, cols].astype(F32) * inverse_query_ref[...])
        ).astype(BF16)
        normed[tokens : 2 * tokens, cols] = (
            gain_key_ref[:, cols] * (key_ref[:, cols].astype(F32) * inverse_key_ref[...])
        ).astype(BF16)

    def pack_qk(group, carry):
        lo = pl.multiple_of(group * 256, 256)
        stacked = normed[:, pl.ds(lo, 256)]
        keys = stacked[tokens : 2 * tokens]
        high = jnp.concatenate([keys[:, 0:HD], keys[:, HD : 2 * HD]], axis=0)

        def block_body(block, inner):
            span = pl.ds(pl.multiple_of(block * 256, 256), 256)
            out = pl.ds(block * 16, 16)
            send_qk[group, out, :, 0:256] = (
                mm(pack_first[span, :], stacked).astype(BF16).reshape(16, TILE, 256)
            )
            send_qk[group, out, :, 256:384] = (
                mm(pack_second[span, :], high).astype(BF16).reshape(16, TILE, HD)
            )
            return inner

        lax.fori_loop(0, blocks, block_body, 0)
        scatter(send_qk.at[group], recv_qk.at[group], QK + group)
        return carry

    lax.fori_loop(0, GROUPS, pack_qk, 0)

    def own_maps(own_axis, message_axis, shape):
        row = iota(shape, own_axis)
        message = iota(shape, message_axis)
        base = (row // SLOT) * TILE
        slot = row % SLOT
        first = ones_where(message == base + slot)
        low = ones_where((message == base + 12 + slot) & (slot < 4))
        high_a = ones_where((message == base + slot - 4) & (slot >= 4))
        high_b = ones_where((message == base + slot + 4) & (slot >= 4))
        labels = ones_where(message == base + 8 + slot - jnp.where(slot < 8, 0, 4))
        return first, low, high_a, high_b, labels

    first, low, high_a, high_b, label_map = own_maps(0, 1, (192, 256))
    second_a = jnp.concatenate([low, high_a], axis=1)
    second_b = jnp.concatenate([low, high_b], axis=1)
    first_t, low_t, high_a_t, high_b_t, _ = own_maps(1, 0, (256, 192))
    back_first = jnp.concatenate([first_t, low_t], axis=1)
    back_second = jnp.concatenate([high_a_t, high_b_t], axis=1)

    wait_recv(recv_value, VALUE)

    def unpack_value(block, carry):
        span = pl.ds(pl.multiple_of(block * 192, 64), 192)
        src = pl.ds(block * 16, 16)
        t = [recv_value[src, :, i * HD : (i + 1) * HD].reshape(256, HD) for i in range(5)]
        stack = lambda *parts: jnp.concatenate(parts, axis=0)
        value_own[0, span, :] = mm(first, t[0]).astype(BF16)
        value_own[1, span, :] = mm(second_a, stack(t[0], t[2])).astype(BF16)
        value_own[2, span, :] = mm(first, t[1]).astype(BF16)
        value_own[3, span, :] = mm(second_b, stack(t[1], t[2])).astype(BF16)
        value_own[4, span, :] = mm(first, t[3]).astype(BF16)
        value_own[5, span, :] = mm(second_a, stack(t[3], t[4])).astype(BF16)
        found = mm(label_map, t[4])
        early = iota((192, 1), 0) % SLOT < 8
        is_zero = jnp.where(early, found[:, 0:1], found[:, 64:65])
        is_one = jnp.where(early, found[:, 1:2], found[:, 65:66])
        spot = iota((192, HD), 1)
        member = jnp.where(
            spot == 0, is_zero, jnp.where(spot == 1, is_one, 1.0 - is_zero - is_one)
        )
        used = spot < 3
        extend_key[span, :] = jnp.where(used, member, 0.0).astype(BF16)
        extend_query[span, :] = jnp.where(used, FAR * (1.0 - member), 0.0).astype(BF16)
        return carry

    lax.fori_loop(0, blocks, unpack_value, 0)

    factor = HD**-0.5
    scale = factor * math.log2(math.e)
    chunk = 256 if own % 256 == 0 else own

    def attention_group(group, carry):
        wait_recv(recv_qk.at[group], QK + group)

        def unpack_body(block, inner):
            span = pl.ds(pl.multiple_of(block * 192, 64), 192)
            src = pl.ds(block * 16, 16)
            both = recv_qk[group, src, :, 0:256].reshape(256, 256)
            high = recv_qk[group, src, :, 256:384].reshape(256, HD)
            q = mm(first, both).astype(BF16)
            query_own[0, span, :] = q[:, 0:HD]
            query_own[1, span, :] = q[:, HD : 2 * HD]
            key_own[0, span, :] = mm(
                second_a, jnp.concatenate([both[:, 0:HD], high], axis=0)
            ).astype(BF16)
            key_own[1, span, :] = mm(
                second_b, jnp.concatenate([both[:, HD : 2 * HD], high], axis=0)
            ).astype(BF16)
            return inner

        lax.fori_loop(0, blocks, unpack_body, 0)

        def head_body(local, inner):
            head = group * 2 + local
            key_sum[local] = jnp.zeros((own, HD), F32)
            value_sum[...] = jnp.zeros((own, HD), F32)
            keys = key_own[local]
            values = value_own[head]
            keys_wide = jnp.concatenate([keys, extend_key[...]], axis=1)
            cols = pl.ds(pl.multiple_of(head * HD, HD), HD)

            def row_body(index, deepest):
                span = pl.ds(pl.multiple_of(index * chunk, chunk), chunk)
                q = query_own[local, span, :]
                cot = cotangent_ref[span, cols]
                scores = mm_nt(jnp.concatenate([q, extend_query[span, :]], axis=1), keys_wide)
                raised = jnp.exp2((scores - jnp.max(scores, axis=1, keepdims=True)) * scale)
                weights = (raised * (1.0 / jnp.sum(raised, axis=1, keepdims=True))).astype(BF16)
                attended = mm(weights, values).astype(BF16)
                attended_ref[span, cols] = attended
                delta = jnp.sum(
                    cot.astype(F32) * attended.astype(F32), axis=1, keepdims=True
                )
                grad_weights = mm_nt(cot, values)
                grad_scores = (weights.astype(F32) * (grad_weights - delta)).astype(BF16)
                grad_query_own[local, span, :] = (mm(grad_scores, keys) * factor).astype(BF16)
                value_sum[...] += mm_tn(weights, cot)
                key_sum[local] += mm_tn(grad_scores, q)
                return deepest

            lax.fori_loop(0, own // chunk, row_body, 0)
            grad_value_own[head] = value_sum[...].astype(BF16)
            return inner

        lax.fori_loop(0, 2, head_body, 0)

        def pack_body(block, inner):
            span = pl.ds(pl.multiple_of(block * 192, 64), 192)
            out = pl.ds(block * 16, 16)
            q_a = grad_query_own[0, span, :]
            q_b = grad_query_own[1, span, :]
            k_a = (key_sum[0, span, :] * factor).astype(BF16)
            k_b = (key_sum[1, span, :] * factor).astype(BF16)
            stacked = jnp.concatenate(
                [jnp.concatenate([q_a, q_b], axis=1), jnp.concatenate([k_a, k_b], axis=1)],
                axis=0,
            )
            back_qk[group, out, :, 0:256] = (
                mm(back_first, stacked).astype(BF16).reshape(16, TILE, 256)
            )
            back_qk[group, out, :, 256:384] = (
                mm(back_second, jnp.concatenate([k_a, k_b], axis=0))
                .astype(BF16)
                .reshape(16, TILE, HD)
            )
            return inner

        lax.fori_loop(0, blocks, pack_body, 0)
        scatter(back_qk.at[group], home_qk.at[group], BACK_QK + group)
        return carry

    lax.fori_loop(0, GROUPS, attention_group, 0)

    def pack_grad_value(block, carry):
        span = pl.ds(pl.multiple_of(block * 192, 64), 192)
        out = pl.ds(block * 16, 16)
        v = [grad_value_own[h, span, :] for h in range(HEADS)]
        stack = lambda *parts: jnp.concatenate(parts, axis=0)

        def put(lo, part):
            back_value[out, :, lo : lo + HD] = part.astype(BF16).reshape(16, TILE, HD)

        put(0, mm(back_first, stack(v[0], v[1])))
        put(128, mm(back_first, stack(v[2], v[3])))
        put(256, mm(back_second, stack(v[1], v[3])))
        put(384, mm(back_first, stack(v[4], v[5])))
        put(512, mm(high_a_t, v[5]))
        return carry

    lax.fori_loop(0, blocks, pack_grad_value, 0)
    scatter(back_value, home_value, BACK_VALUE)

    def unpack_home(group, carry):
        wait_recv(home_qk.at[group], BACK_QK + group)
        both = home_qk[group, :, :, 0:256].reshape(rows, 256)
        high = home_qk[group, :, :, 256:384].reshape(rows, HD)
        lo = pl.multiple_of(group * 256, 256)
        grad_qn[:, pl.ds(lo, 256)] = mm(unpack_first[...], both).astype(BF16)
        keys = mm(unpack_low[...], both)
        grad_kn[:, pl.ds(lo, HD)] = (keys[:, 0:HD] + mm(unpack_high_a[...], high)).astype(BF16)
        grad_kn[:, pl.ds(lo + HD, HD)] = (
            keys[:, HD : 2 * HD] + mm(unpack_high_b[...], high)
        ).astype(BF16)
        return carry

    lax.fori_loop(0, GROUPS, unpack_home, 0)

    near = my_y * size_c + my_c
    near_count = size_y * size_c
    center_q = jnp.zeros((tokens, HD), F32)
    center_k = jnp.zeros((tokens, HD), F32)
    gain_near[near] = jnp.zeros((8, feat), F32)
    for h in range(HEADS):
        cols = slice(h * HD, (h + 1) * HD)
        term = grad_qn[:, cols].astype(F32) * (
            query_ref[:, cols].astype(F32) * inverse_query_ref[...]
        )
        gain_near[near, 0:1, cols] = jnp.sum(term, axis=0, keepdims=True)
        center_q = center_q + gain_query_ref[:, cols] * term
        term = grad_kn[:, cols].astype(F32) * (
            key_ref[:, cols].astype(F32) * inverse_key_ref[...]
        )
        gain_near[near, 1:2, cols] = jnp.sum(term, axis=0, keepdims=True)
        center_k = center_k + gain_key_ref[:, cols] * term
    stat_center[my_x] = jnp.where(
        half,
        jnp.sum(center_q, axis=1, keepdims=True),
        jnp.sum(center_k, axis=1, keepdims=True),
    )
    share(stat_center, my_x, tensors, lambda to: {"tensor": to}, CENTER)
    share(
        gain_near,
        near,
        near_count,
        lambda to: {"dp": ((to // size_c) * size_z + my_z) * size_c + to % size_c},
        NEAR,
    )
    share_wait(stat_center, tensors, CENTER)
    total = stat_center[0]
    for x in range(1, tensors):
        total = total + stat_center[x]
    total = total / feat_total
    center_q = jnp.broadcast_to(total[:, 0:1], (tokens, HD))
    center_k = jnp.broadcast_to(total[:, 64:65], (tokens, HD))
    for h in range(HEADS):
        cols = slice(h * HD, (h + 1) * HD)
        inverse = inverse_query_ref[...]
        unit = query_ref[:, cols].astype(F32) * inverse
        scaled = gain_query_ref[:, cols] * grad_qn[:, cols].astype(F32)
        grad_query_ref[:, cols] = ((scaled - unit * center_q) * inverse).astype(BF16)
        inverse = inverse_key_ref[...]
        unit = key_ref[:, cols].astype(F32) * inverse
        scaled = gain_key_ref[:, cols] * grad_kn[:, cols].astype(F32)
        grad_key_ref[:, cols] = ((scaled - unit * center_k) * inverse).astype(BF16)

    share_wait(gain_near, near_count, NEAR)
    total = gain_near[0]
    for i in range(1, near_count):
        total = total + gain_near[i]
    gain_far[my_z] = total
    share(
        gain_far,
        my_z,
        size_z,
        lambda to: {"dp": (my_y * size_z + to) * size_c + my_c},
        FARTHER,
    )

    wait_recv(home_value, BACK_VALUE)
    t = [home_value[:, :, i * HD : (i + 1) * HD].reshape(rows, HD) for i in range(5)]
    unpacked = (
        mm(unpack_first[...], t[0]),
        mm(unpack_low[...], t[0]) + mm(unpack_high_a[...], t[2]),
        mm(unpack_first[...], t[1]),
        mm(unpack_low[...], t[1]) + mm(unpack_high_b[...], t[2]),
        mm(unpack_first[...], t[3]),
        mm(unpack_low[...], t[3]) + mm(unpack_high_a[...], t[4]),
    )
    for h in range(HEADS):
        grad_value_ref[:, h * HD : (h + 1) * HD] = unpacked[h].astype(BF16)

    share_wait(gain_far, size_z, FARTHER)
    total = gain_far[0]
    for i in range(1, size_z):
        total = total + gain_far[i]
    gain_out_ref[...] = total

    wait_send(send_value, VALUE, dp - 1)
    for group in range(GROUPS):
        wait_send(send_qk.at[group], QK + group, dp - 1)
        wait_send(back_qk.at[group], BACK_QK + group, dp - 1)
    wait_send(back_value, BACK_VALUE, dp - 1)
    wait_send(stat_norm, NORM, tensors - 1)
    wait_send(stat_center, CENTER, tensors - 1)
    wait_send(gain_near, NEAR, near_count - 1)
    wait_send(gain_far, FARTHER, size_z - 1)


def shards(query_raw, key_raw, value_rows, gain_query, gain_key, owner_id, utterance, cotangent):
    dp = lax.axis_size("dp")
    tensors = lax.axis_size("tensor")
    tokens, feat = query_raw.shape
    rows = dp * TILE
    own = dp * SLOT
    _, size_z, _ = SHAPES[dp]
    vmem = pl.BlockSpec(memory_space=pltpu.VMEM)
    out_shape = (
        jax.ShapeDtypeStruct((own, feat), BF16),
        jax.ShapeDtypeStruct((tokens, feat), BF16),
        jax.ShapeDtypeStruct((tokens, feat), BF16),
        jax.ShapeDtypeStruct((tokens, feat), BF16),
        jax.ShapeDtypeStruct((8, feat), F32),
    )
    scratch = [
        pltpu.VMEM((rows, 2 * tokens), BF16),
        pltpu.VMEM((rows, 2 * tokens), BF16),
        pltpu.VMEM((rows, tokens), BF16),
        pltpu.VMEM((tokens, rows), BF16),
        pltpu.VMEM((tokens, rows), BF16),
        pltpu.VMEM((tokens, rows), BF16),
        pltpu.VMEM((tokens, rows), BF16),
        pltpu.VMEM((2 * tokens, feat), BF16),
        pltpu.VMEM((tokens, HD), F32),
        pltpu.VMEM((tokens, HD), F32),
        pltpu.VMEM((dp, TILE, 640), BF16),
        pltpu.VMEM((dp, TILE, 640), BF16),
        pltpu.VMEM((GROUPS, dp, TILE, 384), BF16),
        pltpu.VMEM((GROUPS, dp, TILE, 384), BF16),
        pltpu.VMEM((GROUPS, dp, TILE, 384), BF16),
        pltpu.VMEM((GROUPS, dp, TILE, 384), BF16),
        pltpu.VMEM((dp, TILE, 640), BF16),
        pltpu.VMEM((dp, TILE, 640), BF16),
        pltpu.VMEM((HEADS, own, HD), BF16),
        pltpu.VMEM((HEADS, own, HD), BF16),
        pltpu.VMEM((own, HD), BF16),
        pltpu.VMEM((own, HD), BF16),
        pltpu.VMEM((2, own, HD), BF16),
        pltpu.VMEM((2, own, HD), BF16),
        pltpu.VMEM((2, own, HD), BF16),
        pltpu.VMEM((2, own, HD), F32),
        pltpu.VMEM((own, HD), F32),
        pltpu.VMEM((tokens, feat), BF16),
        pltpu.VMEM((tokens, feat), BF16),
        pltpu.VMEM((tensors, tokens, HD), F32),
        pltpu.VMEM((tensors, tokens, HD), F32),
        pltpu.VMEM((dp // size_z, 8, feat), F32),
        pltpu.VMEM((size_z, 8, feat), F32),
        pltpu.SemaphoreType.DMA((12,)),
        pltpu.SemaphoreType.DMA((12,)),
    ]
    attended, grad_query, grad_key, grad_value, gains = pl.pallas_call(
        functools.partial(kernel, dp, tensors, tokens),
        out_shape=out_shape,
        in_specs=[vmem] * 8,
        out_specs=[vmem] * 5,
        scratch_shapes=scratch,
        compiler_params=pltpu.CompilerParams(
            has_side_effects=True, vmem_limit_bytes=58 * 1024 * 1024
        ),
    )(
        query_raw,
        key_raw,
        value_rows,
        gain_query[None, :],
        gain_key[None, :],
        owner_id[None, :],
        utterance[None, :],
        cotangent,
    )
    return (attended, grad_query, grad_key, grad_value, gains[0], gains[1])


def solution(mesh):
    wide = P("dp", "tensor")
    return jax.shard_map(
        shards,
        mesh=mesh,
        in_specs=(wide, wide, wide, P("tensor"), P("tensor"), P("dp"), P("dp"), wide),
        out_specs=(wide, wide, wide, wide, P("tensor"), P("tensor")),
        check_vma=False,
    )
```

```python
import functools
import math

import jax
import jax.numpy as jnp
from jax import lax
from jax.experimental import pallas as pl
from jax.experimental.pallas import tpu as pltpu
from jax.sharding import PartitionSpec as P

HD = 128
EPSILON = 1e-06
SLOT = 12
TILE = 16
HEADS = 6
GROUPS = 3
FAR = -(2.0**30)
F32 = jnp.float32
BF16 = jnp.bfloat16
MESH = pl.DeviceIdType.MESH
STRIDE = 23
SHAPES = {64: (4, 8, 2), 16: (2, 4, 2)}


def mm(a, b):
    return lax.dot_general(a, b, (((1,), (0,)), ((), ())), preferred_element_type=F32)


def mm_nt(a, b):
    return lax.dot_general(a, b, (((1,), (1,)), ((), ())), preferred_element_type=F32)


def iota(shape, axis):
    return lax.broadcasted_iota(jnp.int32, shape, axis)


def ones_where(mask):
    return jnp.where(mask, 1.0, 0.0).astype(BF16)


def to_i32(x):
    return x.astype(jnp.int32)


def over(*parts):
    return jnp.concatenate(parts, axis=0)


def beside(*parts):
    return jnp.concatenate(parts, axis=1)


def kernel(
    dp,
    tensors,
    tokens,
    query_ref,
    key_ref,
    value_ref,
    gain_query_ref,
    gain_key_ref,
    owner_ref,
    utterance_ref,
    cotangent_hbm,
    attended_hbm,
    grad_query_ref,
    grad_key_ref,
    grad_value_ref,
    gain_query_out,
    gain_key_out,
    pack_first,
    pack_second,
    unpack_first,
    unpack_low,
    unpack_high_a,
    unpack_high_b,
    normed,
    inverse_query_ref,
    inverse_key_ref,
    out_0,
    out_1,
    out_2,
    out_3,
    in_0,
    in_1,
    in_2,
    in_3,
    back_0,
    back_1,
    back_2,
    back_3,
    home_0,
    home_1,
    home_2,
    home_3,
    value_own,
    grad_value_own,
    extend_query,
    extend_key,
    query_own,
    key_own,
    grad_query_own,
    grad_key_own,
    key_sum,
    value_sum,
    grad_qn,
    grad_kn,
    center_query_ref,
    center_key_ref,
    stat_norm,
    stat_center,
    gain_near,
    gain_far,
    cotangent_ref,
    attended_ref,
    send_sems,
    recv_sems,
    local_sems,
):
    size_y, size_z, size_c = SHAPES[dp]
    me = lax.axis_index("dp")
    my_x = lax.axis_index("tensor")
    my_c = me % size_c
    my_z = (me // size_c) % size_z
    my_y = me // (size_c * size_z)
    rows = dp * TILE
    own = dp * SLOT
    feat = HEADS * HD
    feat_total = feat * tensors
    blocks = dp // 16

    def scatter(source, target, index):
        pltpu.make_async_copy(source.at[me], target.at[me], recv_sems.at[index]).start()

        def step_body(step, carry):
            peer = lax.rem(me + step * STRIDE, dp)
            pltpu.make_async_remote_copy(
                src_ref=source.at[peer],
                dst_ref=target.at[me],
                send_sem=send_sems.at[index],
                recv_sem=recv_sems.at[index],
                device_id={"dp": peer},
                device_id_type=MESH,
            ).start()
            return carry

        lax.fori_loop(1, dp, step_body, 0)

    def wait_recv(target, index):
        pltpu.make_async_copy(target, target, recv_sems.at[index]).wait()

    def wait_send(source, index, count):
        part = source.at[pl.ds(0, count)]
        pltpu.make_async_copy(part, part, send_sems.at[index]).wait()

    def share(buffer, slot, count, device_of, index):
        def step_body(step, carry):
            to = lax.rem(slot + step, count)
            pltpu.make_async_remote_copy(
                src_ref=buffer.at[slot],
                dst_ref=buffer.at[slot],
                send_sem=send_sems.at[index],
                recv_sem=recv_sems.at[index],
                device_id=device_of(to),
                device_id_type=MESH,
            ).start()
            return carry

        lax.fori_loop(1, count, step_body, 0)

    def share_wait(buffer, count, index):
        part = buffer.at[pl.ds(0, count - 1)]
        pltpu.make_async_copy(part, part, recv_sems.at[index]).wait()

    OUT, BACK, NORM, CENTER, NEAR, FARTHER = 0, 4, 8, 9, 10, 11

    load_cotangent = pltpu.make_async_copy(cotangent_hbm, cotangent_ref, local_sems.at[0])
    load_cotangent.start()

    half = iota((tokens, HD), 1) < 64
    query_f = query_ref[...].astype(F32)
    key_f = key_ref[...].astype(F32)
    stat_norm[my_x] = jnp.where(
        half,
        jnp.sum(query_f * query_f, axis=1, keepdims=True),
        jnp.sum(key_f * key_f, axis=1, keepdims=True),
    )
    share(stat_norm, my_x, tensors, lambda to: {"tensor": to}, NORM)

    owner_row = owner_ref[...].reshape(1, tokens)
    chosen = jnp.where(iota((dp, tokens), 0) == owner_row, 1.0, 0.0)
    upper = ones_where(iota((tokens, tokens), 0) < iota((tokens, tokens), 1))
    rank_row = jnp.sum(mm(chosen.astype(BF16), upper) * chosen, axis=0, keepdims=True)
    code_row_f = owner_row.astype(F32) * TILE + rank_row
    diagonal = iota((tokens, tokens), 0) == iota((tokens, tokens), 1)

    def as_column(row):
        return jnp.sum(jnp.where(diagonal, row, 0.0), axis=1, keepdims=True)

    rank_row = to_i32(rank_row)
    code_row = to_i32(code_row_f)
    none = -1

    utterance_col = to_i32(as_column(utterance_ref[...].reshape(1, tokens).astype(F32)))
    lane = iota((tokens, HD), 1)
    label_low = ones_where(lane == utterance_col)
    label_high = ones_where(lane == utterance_col + 64)

    def value_head(h):
        return value_ref[:, h * HD : (h + 1) * HD]

    def put(buffer, out, lo, part):
        width = part.shape[1]
        buffer[out, :, lo : lo + width] = part.astype(BF16).reshape(16, TILE, width)

    def pack_0(block, carry):
        span = pl.ds(pl.multiple_of(block * 256, 256), 256)
        out = pl.ds(block * 16, 16)
        row = iota((256, tokens), 0) + block * 256
        first = beside(
            ones_where(row == code_row),
            ones_where(row == jnp.where(rank_row < 4, code_row + 12, none)),
        )
        second = beside(
            ones_where(row == jnp.where(rank_row >= 4, code_row - 4, none)),
            ones_where(row == jnp.where(rank_row >= 4, code_row + 4, none)),
        )
        third = ones_where(row == jnp.where(rank_row < 8, code_row + 8, none))
        pack_first[span, :] = first
        pack_second[span, :] = second
        put(out_0, out, 0, mm(first, over(value_head(0), value_head(1))))
        put(out_0, out, HD, mm(second, over(value_head(1), label_high)) + mm(third, label_low))
        return carry

    lax.fori_loop(0, blocks, pack_0, 0)
    scatter(out_0, in_0, OUT)

    share_wait(stat_norm, tensors, NORM)
    total = stat_norm[0]
    for x in range(1, tensors):
        total = total + stat_norm[x]
    inverse = lax.rsqrt(total / feat_total + EPSILON)
    inverse_query_ref[...] = jnp.broadcast_to(inverse[:, 0:1], (tokens, HD))
    inverse_key_ref[...] = jnp.broadcast_to(inverse[:, 64:65], (tokens, HD))

    def gain_of(ref, h):
        return ref[h * HD : (h + 1) * HD].reshape(1, HD)

    def unit_query(h):
        return query_ref[:, h * HD : (h + 1) * HD].astype(F32) * inverse_query_ref[...]

    def unit_key(h):
        return key_ref[:, h * HD : (h + 1) * HD].astype(F32) * inverse_key_ref[...]

    def pack_qk(group, buffer, index):
        for h in (2 * group, 2 * group + 1):
            cols = slice(h * HD, (h + 1) * HD)
            normed[0:tokens, cols] = (gain_of(gain_query_ref, h) * unit_query(h)).astype(BF16)
            normed[tokens : 2 * tokens, cols] = (
                gain_of(gain_key_ref, h) * unit_key(h)
            ).astype(BF16)
        lo = group * 256

        def block_body(block, carry):
            span = pl.ds(pl.multiple_of(block * 256, 256), 256)
            out = pl.ds(block * 16, 16)
            first = pack_first[span, :]
            second = pack_second[span, :]
            keys = slice(tokens, 2 * tokens)
            put(buffer, out, 0, mm(first, normed[:, lo : lo + 256]))
            high = over(normed[keys, lo : lo + HD], normed[keys, lo + HD : lo + 256])
            put(buffer, out, 256, mm(second, high))
            if group == 1:
                v = [value_head(h) for h in range(HEADS)]
                put(buffer, out, 384, mm(first, over(beside(v[2], v[4]), beside(v[3], v[5]))))
                put(buffer, out, 640, mm(second, over(v[3], v[5])))
            return carry

        lax.fori_loop(0, blocks, block_body, 0)
        scatter(buffer, (in_1, in_2, in_3)[group], index)

    pack_qk(0, out_1, OUT + 1)
    pack_qk(1, out_2, OUT + 2)
    pack_qk(2, out_3, OUT + 3)

    code_col = to_i32(as_column(code_row_f))
    rank_col = code_col % TILE
    column = iota((tokens, rows), 1)
    unpack_first[...] = ones_where(column == code_col)
    unpack_low[...] = ones_where(column == jnp.where(rank_col < 4, code_col + 12, none))
    unpack_high_a[...] = ones_where(column == jnp.where(rank_col >= 4, code_col - 4, none))
    unpack_high_b[...] = ones_where(column == jnp.where(rank_col >= 4, code_col + 4, none))

    def own_maps(own_axis, message_axis, shape):
        row = iota(shape, own_axis)
        message = iota(shape, message_axis)
        base = (row // SLOT) * TILE
        slot = row % SLOT
        first = ones_where(message == base + slot)
        low = ones_where((message == base + 12 + slot) & (slot < 4))
        high_a = ones_where((message == base + slot - 4) & (slot >= 4))
        high_b = ones_where((message == base + slot + 4) & (slot >= 4))
        labels = ones_where(message == base + 8 + slot - jnp.where(slot < 8, 0, 4))
        return first, low, high_a, high_b, labels

    first, low, high_a, high_b, label_map = own_maps(0, 1, (192, 256))
    second_a = beside(low, high_a)
    second_b = beside(low, high_b)
    first_t, low_t, high_a_t, high_b_t, _ = own_maps(1, 0, (256, 192))
    back_first = beside(first_t, low_t)
    back_second = beside(high_a_t, high_b_t)

    def message(buffer, src, tile):
        return buffer[src, :, tile * HD : (tile + 1) * HD].reshape(256, HD)

    wait_recv(in_0, OUT)

    def unpack_0(block, carry):
        span = pl.ds(pl.multiple_of(block * 192, 64), 192)
        src = pl.ds(block * 16, 16)
        t0 = message(in_0, src, 0)
        t1 = message(in_0, src, 1)
        value_own[0, span, :] = mm(first, t0).astype(BF16)
        value_own[1, span, :] = mm(second_a, over(t0, t1)).astype(BF16)
        found = mm(label_map, t1)
        early = iota((192, 1), 0) % SLOT < 8
        is_zero = jnp.where(early, found[:, 0:1], found[:, 64:65])
        is_one = jnp.where(early, found[:, 1:2], found[:, 65:66])
        spot = iota((192, HD), 1)
        member = jnp.where(
            spot == 0, is_zero, jnp.where(spot == 1, is_one, 1.0 - is_zero - is_one)
        )
        used = spot < 3
        extend_key[span, :] = jnp.where(used, member, 0.0).astype(BF16)
        extend_query[span, :] = jnp.where(used, FAR * (1.0 - member), 0.0).astype(BF16)
        return carry

    lax.fori_loop(0, blocks, unpack_0, 0)
    load_cotangent.wait()

    factor = HD**-0.5
    scale = factor * math.log2(math.e)
    chunk = 256 if own % 256 == 0 else own

    def attention_group(group):
        buffer = (in_1, in_2, in_3)[group]
        wait_recv(buffer, OUT + 1 + group)

        def unpack_body(block, carry):
            span = pl.ds(pl.multiple_of(block * 192, 64), 192)
            src = pl.ds(block * 16, 16)
            t0, t1, t2 = (message(buffer, src, i) for i in range(3))
            q = mm(first, beside(t0, t1)).astype(BF16)
            query_own[0, span, :] = q[:, 0:HD]
            query_own[1, span, :] = q[:, HD : 2 * HD]
            key_own[0, span, :] = mm(second_a, over(t0, t2)).astype(BF16)
            key_own[1, span, :] = mm(second_b, over(t1, t2)).astype(BF16)
            if group == 1:
                t0, t1, t2 = (message(buffer, src, i) for i in range(3, 6))
                v = mm(first, beside(t0, t1)).astype(BF16)
                value_own[2, span, :] = v[:, 0:HD]
                value_own[4, span, :] = v[:, HD : 2 * HD]
                value_own[3, span, :] = mm(second_a, over(t0, t2)).astype(BF16)
                value_own[5, span, :] = mm(second_b, over(t1, t2)).astype(BF16)
            return carry

        lax.fori_loop(0, blocks, unpack_body, 0)
        key_sum[...] = jnp.zeros((2, HD, own), F32)
        value_sum[...] = jnp.zeros((2, HD, own), F32)

        def row_body(index, carry):
            span = pl.ds(pl.multiple_of(index * chunk, chunk), chunk)
            for local in range(2):
                head = 2 * group + local
                cols = slice(head * HD, (head + 1) * HD)
                keys = key_own[local]
                values = value_own[head]
                q = query_own[local, span, :]
                cot = cotangent_ref[span, cols]
                scores = mm_nt(beside(q, extend_query[span, :]), beside(keys, extend_key[...]))
                raised = jnp.exp2((scores - jnp.max(scores, axis=1, keepdims=True)) * scale)
                weights = (raised * (1.0 / jnp.sum(raised, axis=1, keepdims=True))).astype(BF16)
                attended = mm(weights, values).astype(BF16)
                attended_ref[span, cols] = attended
                delta = jnp.sum(cot.astype(F32) * attended.astype(F32), axis=1, keepdims=True)
                grad_weights = mm_nt(cot, values)
                grad_scores = (weights.astype(F32) * (grad_weights - delta)).astype(BF16)
                grad_query_own[local, span, :] = (mm(grad_scores, keys) * factor).astype(BF16)
                value_sum[local] += mm(cot.T, weights)
                key_sum[local] += mm(q.T, grad_scores)
            return carry

        lax.fori_loop(0, own // chunk, row_body, 0)
        for local in range(2):
            grad_key_own[local] = (key_sum[local].T * factor).astype(BF16)
            grad_value_own[2 * group + local] = value_sum[local].T.astype(BF16)

        target = (back_0, back_1, back_2)[group]

        def pack_body(block, carry):
            span = pl.ds(pl.multiple_of(block * 192, 64), 192)
            out = pl.ds(block * 16, 16)
            q = beside(grad_query_own[0, span, :], grad_query_own[1, span, :])
            k = [grad_key_own[i, span, :] for i in range(2)]
            put(target, out, 0, mm(back_first, over(q, beside(k[0], k[1]))))
            put(target, out, 256, mm(back_second, over(k[0], k[1])))
            if group == 1:
                v = [grad_value_own[i, span, :] for i in range(4)]
                put(
                    target, out, 384, mm(back_first, over(beside(v[0], v[2]), beside(v[1], v[3])))
                )
                put(target, out, 640, mm(back_second, over(v[1], v[3])))
            return carry

        lax.fori_loop(0, blocks, pack_body, 0)
        scatter(target, (home_0, home_1, home_2)[group], BACK + group)

    for group in range(3):
        attention_group(group)

    def pack_last(block, carry):
        span = pl.ds(pl.multiple_of(block * 192, 64), 192)
        out = pl.ds(block * 16, 16)
        v4 = grad_value_own[4, span, :]
        v5 = grad_value_own[5, span, :]
        put(back_3, out, 0, mm(back_first, over(v4, v5)))
        put(back_3, out, HD, mm(high_a_t, v5))
        return carry

    lax.fori_loop(0, blocks, pack_last, 0)
    scatter(back_3, home_3, BACK + 3)
    save_attended = pltpu.make_async_copy(attended_ref, attended_hbm, local_sems.at[1])
    save_attended.start()

    near = my_y * size_c + my_c
    near_count = size_y * size_c
    center_query_ref[...] = jnp.zeros((tokens, HD), F32)
    center_key_ref[...] = jnp.zeros((tokens, HD), F32)
    gain_near[near] = jnp.zeros((16, HD), F32)

    def home_group(group):
        buffer = (home_0, home_1, home_2)[group]
        wait_recv(buffer, BACK + group)
        tile = lambda i: buffer[:, :, i * HD : (i + 1) * HD].reshape(rows, HD)
        both = beside(tile(0), tile(1))
        queries = mm(unpack_first[...], both)
        keys = mm(unpack_low[...], both)
        high = (mm(unpack_high_a[...], tile(2)), mm(unpack_high_b[...], tile(2)))
        for local in range(2):
            h = 2 * group + local
            cols = slice(h * HD, (h + 1) * HD)
            part = slice(local * HD, (local + 1) * HD)
            grad_q = queries[:, part].astype(BF16)
            grad_k = (keys[:, part] + high[local]).astype(BF16)
            grad_qn[:, cols] = grad_q
            grad_kn[:, cols] = grad_k
            term = grad_q.astype(F32) * unit_query(h)
            gain_near[near, h : h + 1, :] = jnp.sum(term, axis=0, keepdims=True)
            center_query_ref[...] += gain_of(gain_query_ref, h) * term
            term = grad_k.astype(F32) * unit_key(h)
            gain_near[near, 8 + h : 9 + h, :] = jnp.sum(term, axis=0, keepdims=True)
            center_key_ref[...] += gain_of(gain_key_ref, h) * term

    for group in range(3):
        home_group(group)

    stat_center[my_x] = jnp.where(
        half,
        jnp.sum(center_query_ref[...], axis=1, keepdims=True),
        jnp.sum(center_key_ref[...], axis=1, keepdims=True),
    )
    share(stat_center, my_x, tensors, lambda to: {"tensor": to}, CENTER)
    share(
        gain_near,
        near,
        near_count,
        lambda to: {"dp": ((to // size_c) * size_z + my_z) * size_c + to % size_c},
        NEAR,
    )

    def value_home(buffer, start, h):
        tile = lambda i: buffer[:, :, (start + i) * HD : (start + i + 1) * HD].reshape(rows, HD)
        both = beside(tile(0), tile(1))
        evens = mm(unpack_first[...], both)
        odds = mm(unpack_low[...], both)
        high = (mm(unpack_high_a[...], tile(2)), mm(unpack_high_b[...], tile(2)))
        for i in range(2):
            part = slice(i * HD, (i + 1) * HD)
            at = (h + 2 * i) * HD
            grad_value_ref[:, at : at + HD] = evens[:, part].astype(BF16)
            grad_value_ref[:, at + HD : at + 2 * HD] = (odds[:, part] + high[i]).astype(BF16)

    value_home(home_1, 3, 0)

    share_wait(gain_near, near_count, NEAR)
    total = gain_near[0]
    for i in range(1, near_count):
        total = total + gain_near[i]
    gain_far[my_z] = total
    share(
        gain_far,
        my_z,
        size_z,
        lambda to: {"dp": (my_y * size_z + to) * size_c + my_c},
        FARTHER,
    )

    share_wait(stat_center, tensors, CENTER)
    total = stat_center[0]
    for x in range(1, tensors):
        total = total + stat_center[x]
    total = total / feat_total
    center_q = jnp.broadcast_to(total[:, 0:1], (tokens, HD))
    center_k = jnp.broadcast_to(total[:, 64:65], (tokens, HD))
    for h in range(HEADS):
        cols = slice(h * HD, (h + 1) * HD)
        scaled = gain_of(gain_query_ref, h) * grad_qn[:, cols].astype(F32)
        grad_query_ref[:, cols] = (
            (scaled - unit_query(h) * center_q) * inverse_query_ref[...]
        ).astype(BF16)
        scaled = gain_of(gain_key_ref, h) * grad_kn[:, cols].astype(F32)
        grad_key_ref[:, cols] = (
            (scaled - unit_key(h) * center_k) * inverse_key_ref[...]
        ).astype(BF16)

    share_wait(gain_far, size_z, FARTHER)
    total = gain_far[0]
    for i in range(1, size_z):
        total = total + gain_far[i]
    for h in range(HEADS):
        gain_query_out[h * HD : (h + 1) * HD] = total[h : h + 1].reshape(HD)
        gain_key_out[h * HD : (h + 1) * HD] = total[8 + h : 9 + h].reshape(HD)

    wait_recv(home_3, BACK + 3)
    t0, t1 = (home_3[:, :, i * HD : (i + 1) * HD].reshape(rows, HD) for i in range(2))
    grad_value_ref[:, 4 * HD : 5 * HD] = mm(unpack_first[...], t0).astype(BF16)
    grad_value_ref[:, 5 * HD : 6 * HD] = (
        mm(unpack_low[...], t0) + mm(unpack_high_a[...], t1)
    ).astype(BF16)

    save_attended.wait()
    for i, buffer in enumerate((out_0, out_1, out_2, out_3, back_0, back_1, back_2, back_3)):
        wait_send(buffer, OUT + i, dp - 1)
    wait_send(stat_norm, NORM, tensors - 1)
    wait_send(stat_center, CENTER, tensors - 1)
    wait_send(gain_near, NEAR, near_count - 1)
    wait_send(gain_far, FARTHER, size_z - 1)


def copy_out(*refs):
    count = len(refs) // 2
    sources, targets, sems = refs[:count], refs[count : 2 * count], refs[-1]
    copies = [
        pltpu.make_async_copy(source, target, sems.at[i])
        for i, (source, target) in enumerate(zip(sources, targets))
    ]
    for copy in copies:
        copy.start()
    for copy in copies:
        copy.wait()


def shards(query_raw, key_raw, value_rows, gain_query, gain_key, owner_id, utterance, cotangent):
    dp = lax.axis_size("dp")
    tensors = lax.axis_size("tensor")
    tokens, feat = query_raw.shape
    rows = dp * TILE
    own = dp * SLOT
    _, size_z, _ = SHAPES[dp]
    vmem = pl.BlockSpec(memory_space=pltpu.VMEM)
    anywhere = pl.BlockSpec(memory_space=pl.ANY)
    out_shape = (
        jax.ShapeDtypeStruct((own, feat), BF16),
        jax.ShapeDtypeStruct((tokens, feat), BF16),
        jax.ShapeDtypeStruct((tokens, feat), BF16),
        jax.ShapeDtypeStruct((tokens, feat), BF16),
        jax.ShapeDtypeStruct((feat,), F32),
        jax.ShapeDtypeStruct((feat,), F32),
    )
    first_out = [pltpu.VMEM((dp, TILE, width), BF16) for width in (256, 384, 768, 384)]
    last_back = [pltpu.VMEM((dp, TILE, width), BF16) for width in (384, 768, 384, 256)]
    scratch = (
        [
            pltpu.VMEM((rows, 2 * tokens), BF16),
            pltpu.VMEM((rows, 2 * tokens), BF16),
            pltpu.VMEM((tokens, rows), BF16),
            pltpu.VMEM((tokens, rows), BF16),
            pltpu.VMEM((tokens, rows), BF16),
            pltpu.VMEM((tokens, rows), BF16),
            pltpu.VMEM((2 * tokens, feat), BF16),
            pltpu.VMEM((tokens, HD), F32),
            pltpu.VMEM((tokens, HD), F32),
        ]
        + first_out * 2
        + last_back * 2
        + [
            pltpu.VMEM((HEADS, own, HD), BF16),
            pltpu.VMEM((HEADS, own, HD), BF16),
            pltpu.VMEM((own, HD), BF16),
            pltpu.VMEM((own, HD), BF16),
            pltpu.VMEM((2, own, HD), BF16),
            pltpu.VMEM((2, own, HD), BF16),
            pltpu.VMEM((2, own, HD), BF16),
            pltpu.VMEM((2, own, HD), BF16),
            pltpu.VMEM((2, HD, own), F32),
            pltpu.VMEM((2, HD, own), F32),
            pltpu.VMEM((tokens, feat), BF16),
            pltpu.VMEM((tokens, feat), BF16),
            pltpu.VMEM((tokens, HD), F32),
            pltpu.VMEM((tokens, HD), F32),
            pltpu.VMEM((tensors, tokens, HD), F32),
            pltpu.VMEM((tensors, tokens, HD), F32),
            pltpu.VMEM((dp // size_z, 16, HD), F32),
            pltpu.VMEM((size_z, 16, HD), F32),
            pltpu.VMEM((own, feat), BF16),
            pltpu.VMEM((own, feat), BF16),
            pltpu.SemaphoreType.DMA((12,)),
            pltpu.SemaphoreType.DMA((12,)),
            pltpu.SemaphoreType.DMA((2,)),
        ]
    )
    results = pl.pallas_call(
        functools.partial(kernel, dp, tensors, tokens),
        out_shape=out_shape,
        in_specs=[vmem] * 7 + [anywhere],
        out_specs=[anywhere] + [vmem] * 5,
        scratch_shapes=scratch,
        compiler_params=pltpu.CompilerParams(
            has_side_effects=True, vmem_limit_bytes=58 * 1024 * 1024
        ),
    )(
        query_raw,
        key_raw,
        value_rows,
        gain_query,
        gain_key,
        owner_id,
        utterance,
        cotangent,
    )
    return pl.pallas_call(
        copy_out,
        out_shape=out_shape,
        in_specs=[anywhere] * 6,
        out_specs=[anywhere] * 6,
        scratch_shapes=[pltpu.SemaphoreType.DMA((6,))],
        compiler_params=pltpu.CompilerParams(vmem_limit_bytes=58 * 1024 * 1024),
    )(*results)


def solution(mesh):
    wide = P("dp", "tensor")
    return jax.shard_map(
        shards,
        mesh=mesh,
        in_specs=(wide, wide, wide, P("tensor"), P("tensor"), P("dp"), P("dp"), wide),
        out_specs=(wide, wide, wide, wide, P("tensor"), P("tensor")),
        check_vma=False,
    )
```

```python
import functools
import math

import jax
import jax.numpy as jnp
from jax import lax
from jax.experimental import pallas as pl
from jax.experimental.pallas import tpu as pltpu
from jax.sharding import PartitionSpec as P

HD = 128
EPSILON = 1e-06
SLOT = 12
TILE = 16
HEADS = 6
GROUPS = 3
FAR = -(2.0**30)
F32 = jnp.float32
BF16 = jnp.bfloat16
MESH = pl.DeviceIdType.MESH
ORDER = {8: (3, -1, 2, -2, 0, -3, 1, 4), 4: (-1, 1, 0, 2)}
SHAPES = {64: (4, 8, 2), 16: (2, 4, 2)}


def mm(a, b):
    return lax.dot_general(a, b, (((1,), (0,)), ((), ())), preferred_element_type=F32)


def mm_nt(a, b):
    return lax.dot_general(a, b, (((1,), (1,)), ((), ())), preferred_element_type=F32)


def iota(shape, axis):
    return lax.broadcasted_iota(jnp.int32, shape, axis)


def ones_where(mask):
    return jnp.where(mask, 1.0, 0.0).astype(BF16)


def to_i32(x):
    return x.astype(jnp.int32)


def over(*parts):
    return jnp.concatenate(parts, axis=0)


def beside(*parts):
    return jnp.concatenate(parts, axis=1)


def kernel(
    dp,
    tensors,
    tokens,
    query_ref,
    key_ref,
    value_ref,
    gain_query_ref,
    gain_key_ref,
    owner_ref,
    utterance_ref,
    cotangent_hbm,
    attended_hbm,
    grad_query_ref,
    grad_key_ref,
    grad_value_ref,
    gain_query_out,
    gain_key_out,
    pack_first,
    pack_second,
    unpack_first,
    unpack_low,
    unpack_high_a,
    unpack_high_b,
    normed,
    inverse_query_ref,
    inverse_key_ref,
    out_0,
    out_0_lent,
    out_1,
    out_1_lent,
    out_2,
    out_2_lent,
    out_3,
    out_3_lent,
    in_0,
    in_1,
    in_2,
    in_3,
    back_0,
    back_0_lent,
    back_1,
    back_1_lent,
    back_2,
    back_2_lent,
    back_3,
    back_3_lent,
    home_0,
    home_1,
    home_2,
    home_3,
    value_own,
    grad_value_own,
    extend_query,
    extend_key,
    query_own,
    key_own,
    grad_query_own,
    grad_key_own,
    key_sum,
    value_sum,
    grad_qn,
    grad_kn,
    center_query_ref,
    center_key_ref,
    relay_1,
    relay_2,
    relay_3,
    relay_4,
    relay_5,
    relay_6,
    stat_norm,
    stat_center,
    gain_near,
    gain_far,
    cotangent_ref,
    attended_ref,
    send_sems,
    recv_sems,
    local_sems,
):
    size_y, size_z, size_c = SHAPES[dp]
    me = lax.axis_index("dp")
    my_x = lax.axis_index("tensor")
    my_c = me % size_c
    my_z = (me // size_c) % size_z
    my_y = me // (size_c * size_z)
    rows = dp * TILE
    own = dp * SLOT
    feat = HEADS * HD
    feat_total = feat * tensors
    blocks = dp // 16

    chips = size_y * size_z
    my_chip = my_y * size_z + my_z
    half_way, quarter = size_z // 2, size_z // 4
    z_of = {
        step: lax.rem(my_z + step + size_z, size_z) for step in ORDER[size_z] + (-quarter, quarter)
    }
    y_of = [lax.rem(my_y + step, size_y) for step in range(size_y)]

    def put_to(source, target, send_index, recv_index, chip, core):
        pltpu.make_async_remote_copy(
            src_ref=source,
            dst_ref=target,
            send_sem=send_sems.at[send_index],
            recv_sem=recv_sems.at[recv_index],
            device_id={"dp": chip * size_c + core},
            device_id_type=MESH,
        ).start()

    def lend(outgoing, index):
        buffer, lent = outgoing
        put_to(lent, buffer.at[:, my_c], LENT + index, LENT + index, my_chip, 1 - my_c)

    def pair_of(target, chip):
        return target.at[pl.ds(chip * size_c, size_c)]

    def scatter(outgoing, target, index, relay=None):
        buffer, lent = outgoing
        pltpu.make_async_copy(lent, lent, recv_sems.at[LENT + index]).wait()
        if relay is not None:
            for step in range(size_y):
                chip = y_of[step] * size_z + z_of[half_way]
                over_chip = y_of[step] * size_z + z_of[quarter if step % 2 == 0 else -quarter]
                put_to(buffer.at[chip], relay.at[step], index, RELAY + index, over_chip, my_c)
        pltpu.make_async_copy(
            buffer.at[my_chip], pair_of(target, my_chip), recv_sems.at[index]
        ).start()

        def step_body(step, carry):
            for place, step_z in enumerate(ORDER[size_z]):
                chip = lax.rem(my_y + step + place, size_y) * size_z + z_of[step_z]

                def direct(chip=chip):
                    put_to(buffer.at[chip], pair_of(target, my_chip), index, index, chip, my_c)

                if step_z == 0:
                    pl.when(step > 0)(direct)
                elif step_z != half_way or relay is None:
                    direct()
            return carry

        lax.fori_loop(0, size_y, step_body, 0)

    def pass_on(target, index, relay):
        pltpu.make_async_copy(relay, relay, recv_sems.at[RELAY + index]).wait()
        for step in range(size_y):
            ahead = quarter if step % 2 == 0 else -quarter
            origin = y_of[(size_y - step) % size_y] * size_z + z_of[-ahead]
            chip = my_y * size_z + z_of[ahead]
            put_to(relay.at[step], pair_of(target, origin), RELAY + index, index, chip, my_c)

    def wait_recv(target, index):
        pltpu.make_async_copy(target, target, recv_sems.at[index]).wait()

    def wait_send(source, index, count):
        part = source.at[pl.ds(0, count)]
        pltpu.make_async_copy(part, part, send_sems.at[index]).wait()

    def share(buffer, slot, count, device_of, index):
        def step_body(step, carry):
            to = lax.rem(slot + step, count)
            pltpu.make_async_remote_copy(
                src_ref=buffer.at[slot],
                dst_ref=buffer.at[slot],
                send_sem=send_sems.at[index],
                recv_sem=recv_sems.at[index],
                device_id=device_of(to),
                device_id_type=MESH,
            ).start()
            return carry

        lax.fori_loop(1, count, step_body, 0)

    def share_wait(buffer, count, index):
        part = buffer.at[pl.ds(0, count - 1)]
        pltpu.make_async_copy(part, part, recv_sems.at[index]).wait()

    OUT, BACK, LENT, RELAY, NORM, CENTER, NEAR, FARTHER = 0, 4, 8, 16, 24, 25, 26, 27

    barrier = pltpu.get_barrier_semaphore()

    def greet(device_id):
        pl.semaphore_signal(barrier, inc=1, device_id=device_id, device_id_type=MESH)

    def greet_chip(step, carry):
        greet({"dp": lax.rem(me + step * size_c, dp)})
        return carry

    for step in range(1, tensors):
        greet({"tensor": lax.rem(my_x + step, tensors)})
    for step in range(size_y):
        greet({"dp": (y_of[step] * size_z + my_z) * size_c + 1 - my_c})
    lax.fori_loop(1, chips, greet_chip, 0)
    load_cotangent = pltpu.make_async_copy(cotangent_hbm, cotangent_ref, local_sems.at[0])
    load_cotangent.start()

    out_0, out_1, out_2, out_3 = zip(
        (out_0, out_1, out_2, out_3), (out_0_lent, out_1_lent, out_2_lent, out_3_lent)
    )
    back_0, back_1, back_2, back_3 = zip(
        (back_0, back_1, back_2, back_3), (back_0_lent, back_1_lent, back_2_lent, back_3_lent)
    )

    half = iota((tokens, HD), 1) < 64
    query_f = query_ref[...].astype(F32)
    key_f = key_ref[...].astype(F32)
    stat_norm[my_x] = jnp.where(
        half,
        jnp.sum(query_f * query_f, axis=1, keepdims=True),
        jnp.sum(key_f * key_f, axis=1, keepdims=True),
    )
    owner_row = owner_ref[...].reshape(1, tokens)
    chosen = jnp.where(iota((dp, tokens), 0) == owner_row, 1.0, 0.0)
    upper = ones_where(iota((tokens, tokens), 0) < iota((tokens, tokens), 1))
    rank_row = jnp.sum(mm(chosen.astype(BF16), upper) * chosen, axis=0, keepdims=True)
    code_row_f = owner_row.astype(F32) * TILE + rank_row

    def sent_place(peer):
        return lax.rem(peer + my_c, 2) * 8 + lax.div(lax.rem(peer, 16), 2)

    diagonal = iota((tokens, tokens), 0) == iota((tokens, tokens), 1)

    def as_column(row):
        return jnp.sum(jnp.where(diagonal, row, 0.0), axis=1, keepdims=True)

    rank_row = to_i32(rank_row)
    code_row = lax.div(owner_row, 16) * 256 + sent_place(owner_row) * TILE + rank_row
    none = -1

    utterance_col = to_i32(as_column(utterance_ref[...].reshape(1, tokens).astype(F32)))
    lane = iota((tokens, HD), 1)
    label_low = ones_where(lane == utterance_col)
    label_high = ones_where(lane == utterance_col + 64)

    def value_head(h):
        return value_ref[:, h * HD : (h + 1) * HD]

    def put(outgoing, block, lo, part):
        buffer, lent = outgoing
        width = part.shape[1]
        part = part.astype(BF16)
        out = pl.ds(block * 8, 8)
        buffer[out, my_c, :, lo : lo + width] = part[0:128].reshape(8, TILE, width)
        lent[out, :, lo : lo + width] = part[128:256].reshape(8, TILE, width)

    def pack_0(block, carry):
        span = pl.ds(pl.multiple_of(block * 256, 256), 256)
        row = iota((256, tokens), 0) + block * 256
        first = beside(
            ones_where(row == code_row),
            ones_where(row == jnp.where(rank_row < 4, code_row + 12, none)),
        )
        second = beside(
            ones_where(row == jnp.where(rank_row >= 4, code_row - 4, none)),
            ones_where(row == jnp.where(rank_row >= 4, code_row + 4, none)),
        )
        third = ones_where(row == jnp.where(rank_row < 8, code_row + 8, none))
        pack_first[span, :] = first
        pack_second[span, :] = second
        put(out_0, block, 0, mm(first, over(value_head(0), value_head(1))))
        put(out_0, block, HD, mm(second, over(value_head(1), label_high)) + mm(third, label_low))
        return carry

    lax.fori_loop(0, blocks, pack_0, 0)
    pl.semaphore_wait(barrier, chips - 1 + tensors - 1 + size_y)
    share(stat_norm, my_x, tensors, lambda to: {"tensor": to}, NORM)
    lend(out_0, OUT)

    code_col = to_i32(as_column(code_row_f))
    rank_col = code_col % TILE
    column = iota((tokens, rows), 1)
    unpack_first[...] = ones_where(column == code_col)
    unpack_low[...] = ones_where(column == jnp.where(rank_col < 4, code_col + 12, none))
    unpack_high_a[...] = ones_where(column == jnp.where(rank_col >= 4, code_col - 4, none))
    unpack_high_b[...] = ones_where(column == jnp.where(rank_col >= 4, code_col + 4, none))

    scatter(out_0, in_0, OUT)
    share_wait(stat_norm, tensors, NORM)
    total = stat_norm[0]
    for x in range(1, tensors):
        total = total + stat_norm[x]
    inverse = lax.rsqrt(total / feat_total + EPSILON)
    inverse_query_ref[...] = jnp.broadcast_to(inverse[:, 0:1], (tokens, HD))
    inverse_key_ref[...] = jnp.broadcast_to(inverse[:, 64:65], (tokens, HD))

    def gain_of(ref, h):
        return ref[h * HD : (h + 1) * HD].reshape(1, HD)

    def unit_query(h):
        return query_ref[:, h * HD : (h + 1) * HD].astype(F32) * inverse_query_ref[...]

    def unit_key(h):
        return key_ref[:, h * HD : (h + 1) * HD].astype(F32) * inverse_key_ref[...]

    def pack_qk(group, buffer, index):
        for h in (2 * group, 2 * group + 1):
            cols = slice(h * HD, (h + 1) * HD)
            normed[0:tokens, cols] = (gain_of(gain_query_ref, h) * unit_query(h)).astype(BF16)
            normed[tokens : 2 * tokens, cols] = (
                gain_of(gain_key_ref, h) * unit_key(h)
            ).astype(BF16)
        lo = group * 256

        def block_body(block, carry):
            span = pl.ds(pl.multiple_of(block * 256, 256), 256)
            first = pack_first[span, :]
            second = pack_second[span, :]
            keys = slice(tokens, 2 * tokens)
            put(buffer, block, 0, mm(first, normed[:, lo : lo + 256]))
            high = over(normed[keys, lo : lo + HD], normed[keys, lo + HD : lo + 256])
            put(buffer, block, 256, mm(second, high))
            if group == 1:
                v = [value_head(h) for h in range(HEADS)]
                put(buffer, block, 384, mm(first, over(beside(v[2], v[4]), beside(v[3], v[5]))))
                put(buffer, block, 640, mm(second, over(v[3], v[5])))
            return carry

        lax.fori_loop(0, blocks, block_body, 0)
        lend(buffer, index)

    pack_qk(0, out_1, OUT + 1)
    pack_qk(1, out_2, OUT + 2)
    scatter(out_1, in_1, OUT + 1, relay_1)
    pack_qk(2, out_3, OUT + 3)
    scatter(out_2, in_2, OUT + 2, relay_2)
    pass_on(in_1, OUT + 1, relay_1)
    scatter(out_3, in_3, OUT + 3, relay_3)

    def own_maps(own_axis, message_axis, shape, place_of):
        row = iota(shape, own_axis)
        message = iota(shape, message_axis)
        device = lax.div(row, SLOT)
        base = place_of(device) * TILE
        slot = row - device * SLOT
        first = ones_where(message == base + slot)
        low = ones_where((message == base + 12 + slot) & (slot < 4))
        high_a = ones_where((message == base + slot - 4) & (slot >= 4))
        high_b = ones_where((message == base + slot + 4) & (slot >= 4))
        labels = ones_where(message == base + 8 + slot - jnp.where(slot < 8, 0, 4))
        return first, low, high_a, high_b, labels

    first, low, high_a, high_b, label_map = own_maps(0, 1, (192, 256), lambda device: device)
    second_a = beside(low, high_a)
    second_b = beside(low, high_b)
    first_t, low_t, high_a_t, high_b_t, _ = own_maps(1, 0, (256, 192), sent_place)
    back_first = beside(first_t, low_t)
    back_second = beside(high_a_t, high_b_t)

    def message(buffer, src, tile):
        return buffer[src, :, tile * HD : (tile + 1) * HD].reshape(256, HD)

    wait_recv(in_0, OUT)

    def unpack_0(block, carry):
        span = pl.ds(pl.multiple_of(block * 192, 64), 192)
        src = pl.ds(block * 16, 16)
        t0 = message(in_0, src, 0)
        t1 = message(in_0, src, 1)
        value_own[0, span, :] = mm(first, t0).astype(BF16)
        value_own[1, span, :] = mm(second_a, over(t0, t1)).astype(BF16)
        found = mm(label_map, t1)
        early = iota((192, 1), 0) % SLOT < 8
        is_zero = jnp.where(early, found[:, 0:1], found[:, 64:65])
        is_one = jnp.where(early, found[:, 1:2], found[:, 65:66])
        spot = iota((192, HD), 1)
        member = jnp.where(
            spot == 0, is_zero, jnp.where(spot == 1, is_one, 1.0 - is_zero - is_one)
        )
        used = spot < 3
        extend_key[span, :] = jnp.where(used, member, 0.0).astype(BF16)
        extend_query[span, :] = jnp.where(used, FAR * (1.0 - member), 0.0).astype(BF16)
        return carry

    lax.fori_loop(0, blocks, unpack_0, 0)
    load_cotangent.wait()

    factor = HD**-0.5
    scale = factor * math.log2(math.e)
    chunk = 256 if own % 256 == 0 else own

    def attention_group(group):
        buffer = (in_1, in_2, in_3)[group]
        wait_recv(buffer, OUT + 1 + group)

        def unpack_body(block, carry):
            span = pl.ds(pl.multiple_of(block * 192, 64), 192)
            src = pl.ds(block * 16, 16)
            t0, t1, t2 = (message(buffer, src, i) for i in range(3))
            q = mm(first, beside(t0, t1)).astype(BF16)
            query_own[0, span, :] = q[:, 0:HD]
            query_own[1, span, :] = q[:, HD : 2 * HD]
            key_own[0, span, :] = mm(second_a, over(t0, t2)).astype(BF16)
            key_own[1, span, :] = mm(second_b, over(t1, t2)).astype(BF16)
            if group == 1:
                t0, t1, t2 = (message(buffer, src, i) for i in range(3, 6))
                v = mm(first, beside(t0, t1)).astype(BF16)
                value_own[2, span, :] = v[:, 0:HD]
                value_own[4, span, :] = v[:, HD : 2 * HD]
                value_own[3, span, :] = mm(second_a, over(t0, t2)).astype(BF16)
                value_own[5, span, :] = mm(second_b, over(t1, t2)).astype(BF16)
            return carry

        lax.fori_loop(0, blocks, unpack_body, 0)
        key_sum[...] = jnp.zeros((2, HD, own), F32)
        value_sum[...] = jnp.zeros((2, HD, own), F32)

        def row_body(index, carry):
            span = pl.ds(pl.multiple_of(index * chunk, chunk), chunk)
            for local in range(2):
                head = 2 * group + local
                cols = slice(head * HD, (head + 1) * HD)
                keys = key_own[local]
                values = value_own[head]
                q = query_own[local, span, :]
                cot = cotangent_ref[span, cols]
                scores = mm_nt(beside(q, extend_query[span, :]), beside(keys, extend_key[...]))
                raised = jnp.exp2((scores - jnp.max(scores, axis=1, keepdims=True)) * scale)
                weights = (raised * (1.0 / jnp.sum(raised, axis=1, keepdims=True))).astype(BF16)
                attended = mm(weights, values).astype(BF16)
                attended_ref[span, cols] = attended
                delta = jnp.sum(cot.astype(F32) * attended.astype(F32), axis=1, keepdims=True)
                grad_weights = mm_nt(cot, values)
                grad_scores = (weights.astype(F32) * (grad_weights - delta)).astype(BF16)
                grad_query_own[local, span, :] = (mm(grad_scores, keys) * factor).astype(BF16)
                value_sum[local] += mm(cot.T, weights)
                key_sum[local] += mm(q.T, grad_scores)
            return carry

        lax.fori_loop(0, own // chunk, row_body, 0)
        for local in range(2):
            grad_key_own[local] = (key_sum[local].T * factor).astype(BF16)
            grad_value_own[2 * group + local] = value_sum[local].T.astype(BF16)

        target = (back_0, back_1, back_2)[group]

        def pack_body(block, carry):
            span = pl.ds(pl.multiple_of(block * 192, 64), 192)
            q = beside(grad_query_own[0, span, :], grad_query_own[1, span, :])
            k = [grad_key_own[i, span, :] for i in range(2)]
            put(target, block, 0, mm(back_first, over(q, beside(k[0], k[1]))))
            put(target, block, 256, mm(back_second, over(k[0], k[1])))
            if group == 1:
                v = [grad_value_own[i, span, :] for i in range(4)]
                put(
                    target, block, 384, mm(back_first, over(beside(v[0], v[2]), beside(v[1], v[3])))
                )
                put(target, block, 640, mm(back_second, over(v[1], v[3])))
            return carry

        lax.fori_loop(0, blocks, pack_body, 0)
        lend(target, BACK + group)
        home = (home_0, home_1, home_2)[group]
        scatter(target, home, BACK + group, (relay_4, relay_5, relay_6)[group])

    attention_group(0)
    pass_on(in_2, OUT + 2, relay_2)
    attention_group(1)
    pass_on(in_3, OUT + 3, relay_3)
    attention_group(2)

    def pack_last(block, carry):
        span = pl.ds(pl.multiple_of(block * 192, 64), 192)
        v4 = grad_value_own[4, span, :]
        v5 = grad_value_own[5, span, :]
        put(back_3, block, 0, mm(back_first, over(v4, v5)))
        put(back_3, block, HD, mm(high_a_t, v5))
        return carry

    lax.fori_loop(0, blocks, pack_last, 0)
    lend(back_3, BACK + 3)
    scatter(back_3, home_3, BACK + 3)
    save_attended = pltpu.make_async_copy(attended_ref, attended_hbm, local_sems.at[1])
    save_attended.start()

    near = my_y * size_c + my_c
    near_count = size_y * size_c
    center_query_ref[...] = jnp.zeros((tokens, HD), F32)
    center_key_ref[...] = jnp.zeros((tokens, HD), F32)
    gain_near[near] = jnp.zeros((16, HD), F32)

    def home_group(group):
        buffer = (home_0, home_1, home_2)[group]
        wait_recv(buffer, BACK + group)
        tile = lambda i: buffer[:, :, i * HD : (i + 1) * HD].reshape(rows, HD)
        both = beside(tile(0), tile(1))
        queries = mm(unpack_first[...], both)
        keys = mm(unpack_low[...], both)
        high = (mm(unpack_high_a[...], tile(2)), mm(unpack_high_b[...], tile(2)))
        for local in range(2):
            h = 2 * group + local
            cols = slice(h * HD, (h + 1) * HD)
            part = slice(local * HD, (local + 1) * HD)
            grad_q = queries[:, part].astype(BF16)
            grad_k = (keys[:, part] + high[local]).astype(BF16)
            grad_qn[:, cols] = grad_q
            grad_kn[:, cols] = grad_k
            term = grad_q.astype(F32) * unit_query(h)
            gain_near[near, h : h + 1, :] = jnp.sum(term, axis=0, keepdims=True)
            center_query_ref[...] += gain_of(gain_query_ref, h) * term
            term = grad_k.astype(F32) * unit_key(h)
            gain_near[near, 8 + h : 9 + h, :] = jnp.sum(term, axis=0, keepdims=True)
            center_key_ref[...] += gain_of(gain_key_ref, h) * term

    pass_on(home_0, BACK, relay_4)
    pass_on(home_1, BACK + 1, relay_5)
    home_group(0)
    home_group(1)
    pass_on(home_2, BACK + 2, relay_6)
    home_group(2)

    stat_center[my_x] = jnp.where(
        half,
        jnp.sum(center_query_ref[...], axis=1, keepdims=True),
        jnp.sum(center_key_ref[...], axis=1, keepdims=True),
    )
    share(stat_center, my_x, tensors, lambda to: {"tensor": to}, CENTER)
    share(
        gain_near,
        near,
        near_count,
        lambda to: {"dp": ((to // size_c) * size_z + my_z) * size_c + to % size_c},
        NEAR,
    )

    def value_home(buffer, start, h):
        tile = lambda i: buffer[:, :, (start + i) * HD : (start + i + 1) * HD].reshape(rows, HD)
        both = beside(tile(0), tile(1))
        evens = mm(unpack_first[...], both)
        odds = mm(unpack_low[...], both)
        high = (mm(unpack_high_a[...], tile(2)), mm(unpack_high_b[...], tile(2)))
        for i in range(2):
            part = slice(i * HD, (i + 1) * HD)
            at = (h + 2 * i) * HD
            grad_value_ref[:, at : at + HD] = evens[:, part].astype(BF16)
            grad_value_ref[:, at + HD : at + 2 * HD] = (odds[:, part] + high[i]).astype(BF16)

    value_home(home_1, 3, 0)

    share_wait(gain_near, near_count, NEAR)
    total = gain_near[0]
    for i in range(1, near_count):
        total = total + gain_near[i]
    gain_far[my_z] = total
    share(
        gain_far,
        my_z,
        size_z,
        lambda to: {"dp": (my_y * size_z + to) * size_c + my_c},
        FARTHER,
    )

    share_wait(stat_center, tensors, CENTER)
    total = stat_center[0]
    for x in range(1, tensors):
        total = total + stat_center[x]
    total = total / feat_total
    center_q = jnp.broadcast_to(total[:, 0:1], (tokens, HD))
    center_k = jnp.broadcast_to(total[:, 64:65], (tokens, HD))
    for h in range(HEADS):
        cols = slice(h * HD, (h + 1) * HD)
        scaled = gain_of(gain_query_ref, h) * grad_qn[:, cols].astype(F32)
        grad_query_ref[:, cols] = (
            (scaled - unit_query(h) * center_q) * inverse_query_ref[...]
        ).astype(BF16)
        scaled = gain_of(gain_key_ref, h) * grad_kn[:, cols].astype(F32)
        grad_key_ref[:, cols] = (
            (scaled - unit_key(h) * center_k) * inverse_key_ref[...]
        ).astype(BF16)

    share_wait(gain_far, size_z, FARTHER)
    total = gain_far[0]
    for i in range(1, size_z):
        total = total + gain_far[i]
    for h in range(HEADS):
        gain_query_out[h * HD : (h + 1) * HD] = total[h : h + 1].reshape(HD)
        gain_key_out[h * HD : (h + 1) * HD] = total[8 + h : 9 + h].reshape(HD)

    wait_recv(home_3, BACK + 3)
    t0, t1 = (home_3[:, :, i * HD : (i + 1) * HD].reshape(rows, HD) for i in range(2))
    grad_value_ref[:, 4 * HD : 5 * HD] = mm(unpack_first[...], t0).astype(BF16)
    grad_value_ref[:, 5 * HD : 6 * HD] = (
        mm(unpack_low[...], t0) + mm(unpack_high_a[...], t1)
    ).astype(BF16)

    save_attended.wait()
    outgoing = (out_0, out_1, out_2, out_3, back_0, back_1, back_2, back_3)
    for i, (buffer, lent) in enumerate(outgoing):
        wait_send(buffer, OUT + i, chips - 1)
        wait_send(lent, LENT + i, chips)
    for i, buffer in enumerate((relay_1, relay_2, relay_3, relay_4, relay_5, relay_6)):
        wait_send(buffer, RELAY + 1 + i, size_y)
    wait_send(stat_norm, NORM, tensors - 1)
    wait_send(stat_center, CENTER, tensors - 1)
    wait_send(gain_near, NEAR, near_count - 1)
    wait_send(gain_far, FARTHER, size_z - 1)


def copy_out(*refs):
    count = (len(refs) - 2) // 3
    sources, targets, held = (refs[i * count : (i + 1) * count] for i in range(3))
    load_sems, save_sems = refs[-2:]
    loads = [
        pltpu.make_async_copy(sources[i], held[i], load_sems.at[i]) for i in range(count)
    ]
    saves = [
        pltpu.make_async_copy(held[i], targets[i], save_sems.at[i]) for i in range(count)
    ]
    for load in loads:
        load.start()
    for load, save in zip(loads, saves):
        load.wait()
        save.start()
    for save in saves:
        save.wait()


def shards(query_raw, key_raw, value_rows, gain_query, gain_key, owner_id, utterance, cotangent):
    dp = lax.axis_size("dp")
    tensors = lax.axis_size("tensor")
    tokens, feat = query_raw.shape
    rows = dp * TILE
    own = dp * SLOT
    size_y, size_z, _ = SHAPES[dp]
    vmem = pl.BlockSpec(memory_space=pltpu.VMEM)
    anywhere = pl.BlockSpec(memory_space=pl.ANY)
    out_shape = (
        jax.ShapeDtypeStruct((own, feat), BF16),
        jax.ShapeDtypeStruct((tokens, feat), BF16),
        jax.ShapeDtypeStruct((tokens, feat), BF16),
        jax.ShapeDtypeStruct((tokens, feat), BF16),
        jax.ShapeDtypeStruct((feat,), F32),
        jax.ShapeDtypeStruct((feat,), F32),
    )
    chips = dp // 2

    def outgoing(*widths):
        shapes = [
            shape for w in widths for shape in ((chips, 2, TILE, w), (chips, TILE, w))
        ]
        return [pltpu.VMEM(shape, BF16) for shape in shapes]

    def incoming(*widths):
        return [pltpu.VMEM((dp, TILE, width), BF16) for width in widths]

    scratch = (
        [
            pltpu.VMEM((rows, 2 * tokens), BF16),
            pltpu.VMEM((rows, 2 * tokens), BF16),
            pltpu.VMEM((tokens, rows), BF16),
            pltpu.VMEM((tokens, rows), BF16),
            pltpu.VMEM((tokens, rows), BF16),
            pltpu.VMEM((tokens, rows), BF16),
            pltpu.VMEM((2 * tokens, feat), BF16),
            pltpu.VMEM((tokens, HD), F32),
            pltpu.VMEM((tokens, HD), F32),
        ]
        + outgoing(256, 384, 768, 384)
        + incoming(256, 384, 768, 384)
        + outgoing(384, 768, 384, 256)
        + incoming(384, 768, 384, 256)
        + [
            pltpu.VMEM((HEADS, own, HD), BF16),
            pltpu.VMEM((HEADS, own, HD), BF16),
            pltpu.VMEM((own, HD), BF16),
            pltpu.VMEM((own, HD), BF16),
            pltpu.VMEM((2, own, HD), BF16),
            pltpu.VMEM((2, own, HD), BF16),
            pltpu.VMEM((2, own, HD), BF16),
            pltpu.VMEM((2, own, HD), BF16),
            pltpu.VMEM((2, HD, own), F32),
            pltpu.VMEM((2, HD, own), F32),
            pltpu.VMEM((tokens, feat), BF16),
            pltpu.VMEM((tokens, feat), BF16),
            pltpu.VMEM((tokens, HD), F32),
            pltpu.VMEM((tokens, HD), F32),
        ]
        + [pltpu.VMEM((size_y, 2, TILE, width), BF16) for width in (384, 768, 384) * 2]
        + [
            pltpu.VMEM((tensors, tokens, HD), F32),
            pltpu.VMEM((tensors, tokens, HD), F32),
            pltpu.VMEM((dp // size_z, 16, HD), F32),
            pltpu.VMEM((size_z, 16, HD), F32),
            pltpu.VMEM((own, feat), BF16),
            pltpu.VMEM((own, feat), BF16),
            pltpu.SemaphoreType.DMA((28,)),
            pltpu.SemaphoreType.DMA((28,)),
            pltpu.SemaphoreType.DMA((2,)),
        ]
    )
    results = pl.pallas_call(
        functools.partial(kernel, dp, tensors, tokens),
        out_shape=out_shape,
        in_specs=[vmem] * 7 + [anywhere],
        out_specs=[anywhere] + [vmem] * 5,
        scratch_shapes=scratch,
        compiler_params=pltpu.CompilerParams(
            collective_id=0, has_side_effects=True, vmem_limit_bytes=58 * 1024 * 1024
        ),
    )(
        query_raw,
        key_raw,
        value_rows,
        gain_query,
        gain_key,
        owner_id,
        utterance,
        cotangent,
    )
    return pl.pallas_call(
        copy_out,
        out_shape=out_shape,
        in_specs=[anywhere] * 6,
        out_specs=[anywhere] * 6,
        scratch_shapes=[pltpu.VMEM(out.shape, out.dtype) for out in out_shape]
        + [pltpu.SemaphoreType.DMA((6,)), pltpu.SemaphoreType.DMA((6,))],
        compiler_params=pltpu.CompilerParams(vmem_limit_bytes=58 * 1024 * 1024),
    )(*results)


def solution(mesh):
    wide = P("dp", "tensor")
    return jax.shard_map(
        shards,
        mesh=mesh,
        in_specs=(wide, wide, wide, P("tensor"), P("tensor"), P("dp"), P("dp"), wide),
        out_specs=(wide, wide, wide, wide, P("tensor"), P("tensor")),
        check_vma=False,
    )
```

```python
import functools
import math

import jax
import jax.numpy as jnp
from jax import lax
from jax.experimental import pallas as pl
from jax.experimental.pallas import tpu as pltpu
from jax.sharding import PartitionSpec as P

HD = 128
EPSILON = 1e-06
SLOT = 12
TILE = 16
HEADS = 6
GROUPS = 3
FAR = -(2.0**30)
F32 = jnp.float32
BF16 = jnp.bfloat16
MESH = pl.DeviceIdType.MESH
ORDER = {8: (3, -1, 2, -2, 0, -3, 1, 4), 4: (-1, 1, 0, 2)}
SHAPES = {64: (4, 8, 2), 16: (2, 4, 2)}


def mm(a, b):
    return lax.dot_general(a, b, (((1,), (0,)), ((), ())), preferred_element_type=F32)


def mm_nt(a, b):
    return lax.dot_general(a, b, (((1,), (1,)), ((), ())), preferred_element_type=F32)


def iota(shape, axis):
    return lax.broadcasted_iota(jnp.int32, shape, axis)


def ones_where(mask):
    return jnp.where(mask, 1.0, 0.0).astype(BF16)


def to_i32(x):
    return x.astype(jnp.int32)


def over(*parts):
    return jnp.concatenate(parts, axis=0)


def beside(*parts):
    return jnp.concatenate(parts, axis=1)


def kernel(
    dp,
    tensors,
    tokens,
    query_ref,
    key_ref,
    value_ref,
    gain_query_ref,
    gain_key_ref,
    owner_ref,
    utterance_ref,
    cotangent_hbm,
    attended_hbm,
    grad_query_ref,
    grad_key_ref,
    grad_value_ref,
    gain_query_out,
    gain_key_out,
    pack_first,
    pack_second,
    unpack_first,
    unpack_low,
    unpack_high_a,
    unpack_high_b,
    normed,
    inverse_query_ref,
    inverse_key_ref,
    out_0,
    out_0_lent,
    out_1,
    out_1_lent,
    out_2,
    out_2_lent,
    out_3,
    out_3_lent,
    in_0,
    in_1,
    in_2,
    in_3,
    back_0,
    back_0_lent,
    back_1,
    back_1_lent,
    back_2,
    back_2_lent,
    back_3,
    back_3_lent,
    home_0,
    home_1,
    home_2,
    home_3,
    value_own,
    grad_value_own,
    extend_query,
    extend_key,
    query_own,
    key_own,
    grad_query_own,
    grad_key_own,
    key_sum,
    value_sum,
    grad_qn,
    grad_kn,
    center_query_ref,
    center_key_ref,
    stat_norm,
    stat_center,
    gain_near,
    gain_far,
    cotangent_ref,
    attended_ref,
    send_sems,
    recv_sems,
    local_sems,
):
    size_y, size_z, size_c = SHAPES[dp]
    me = lax.axis_index("dp")
    my_x = lax.axis_index("tensor")
    my_c = me % size_c
    my_z = (me // size_c) % size_z
    my_y = me // (size_c * size_z)
    rows = dp * TILE
    own = dp * SLOT
    feat = HEADS * HD
    feat_total = feat * tensors
    blocks = dp // 16

    chips = size_y * size_z
    my_chip = my_y * size_z + my_z
    way = 1 - 2 * my_c
    z_of = {step: lax.rem(my_z + way * step + size_z, size_z) for step in ORDER[size_z]}
    y_of = [lax.rem(my_y + step, size_y) for step in range(size_y)]

    def put_to(source, target, send_index, recv_index, chip, core):
        pltpu.make_async_remote_copy(
            src_ref=source,
            dst_ref=target,
            send_sem=send_sems.at[send_index],
            recv_sem=recv_sems.at[recv_index],
            device_id={"dp": chip * size_c + core},
            device_id_type=MESH,
        ).start()

    def lend(outgoing, index):
        buffer, lent = outgoing
        put_to(lent, buffer.at[:, my_c], LENT + index, LENT + index, my_chip, 1 - my_c)

    def pair_of(target, chip):
        return target.at[pl.ds(chip * size_c, size_c)]

    def settle(outgoing, target, index):
        buffer, lent = outgoing
        pltpu.make_async_copy(lent, lent, recv_sems.at[LENT + index]).wait()
        pltpu.make_async_copy(
            buffer.at[my_chip], pair_of(target, my_chip), recv_sems.at[index]
        ).start()

    def send_part(outgoing, target, index, step):
        buffer, _ = outgoing
        for place, step_z in enumerate(ORDER[size_z]):
            chip = lax.rem(my_y + step + place, size_y) * size_z + z_of[step_z]

            def send(chip=chip):
                put_to(buffer.at[chip], pair_of(target, my_chip), index, index, chip, my_c)

            if step_z == 0:
                pl.when(step > 0)(send)
            else:
                send()

    def send_parts(outgoing, target, index, start, stop):
        def body(step, carry):
            send_part(outgoing, target, index, step)
            return carry

        lax.fori_loop(start, stop, body, 0)

    def scatter(outgoing, target, index):
        settle(outgoing, target, index)
        send_parts(outgoing, target, index, 0, size_y)

    def wait_recv(target, index):
        pltpu.make_async_copy(target, target, recv_sems.at[index]).wait()

    def wait_send(source, index, count):
        part = source.at[pl.ds(0, count)]
        pltpu.make_async_copy(part, part, send_sems.at[index]).wait()

    def share(buffer, slot, count, device_of, index):
        def step_body(step, carry):
            to = lax.rem(slot + step, count)
            pltpu.make_async_remote_copy(
                src_ref=buffer.at[slot],
                dst_ref=buffer.at[slot],
                send_sem=send_sems.at[index],
                recv_sem=recv_sems.at[index],
                device_id=device_of(to),
                device_id_type=MESH,
            ).start()
            return carry

        lax.fori_loop(1, count, step_body, 0)

    def share_wait(buffer, count, index):
        part = buffer.at[pl.ds(0, count - 1)]
        pltpu.make_async_copy(part, part, recv_sems.at[index]).wait()

    OUT, BACK, LENT, NORM, CENTER, NEAR, FARTHER = 0, 4, 8, 16, 17, 18, 19

    barrier = pltpu.get_barrier_semaphore()

    def greet(device_id):
        pl.semaphore_signal(barrier, inc=1, device_id=device_id, device_id_type=MESH)

    def greet_chip(step, carry):
        greet({"dp": lax.rem(me + step * size_c, dp)})
        return carry

    for step in range(1, tensors):
        greet({"tensor": lax.rem(my_x + step, tensors)})
    for step in range(size_y):
        greet({"dp": (y_of[step] * size_z + my_z) * size_c + 1 - my_c})
    lax.fori_loop(1, chips, greet_chip, 0)
    load_cotangent = pltpu.make_async_copy(cotangent_hbm, cotangent_ref, local_sems.at[0])
    load_cotangent.start()

    out_0, out_1, out_2, out_3 = zip(
        (out_0, out_1, out_2, out_3), (out_0_lent, out_1_lent, out_2_lent, out_3_lent)
    )
    back_0, back_1, back_2, back_3 = zip(
        (back_0, back_1, back_2, back_3), (back_0_lent, back_1_lent, back_2_lent, back_3_lent)
    )

    half = iota((tokens, HD), 1) < 64
    query_f = query_ref[...].astype(F32)
    key_f = key_ref[...].astype(F32)
    stat_norm[my_x] = jnp.where(
        half,
        jnp.sum(query_f * query_f, axis=1, keepdims=True),
        jnp.sum(key_f * key_f, axis=1, keepdims=True),
    )
    owner_row = owner_ref[...].reshape(1, tokens)
    chosen = jnp.where(iota((dp, tokens), 0) == owner_row, 1.0, 0.0)
    upper = ones_where(iota((tokens, tokens), 0) < iota((tokens, tokens), 1))
    rank_row = jnp.sum(mm(chosen.astype(BF16), upper) * chosen, axis=0, keepdims=True)
    code_row_f = owner_row.astype(F32) * TILE + rank_row

    def sent_place(peer):
        return lax.rem(peer + my_c, 2) * 8 + lax.div(lax.rem(peer, 16), 2)

    diagonal = iota((tokens, tokens), 0) == iota((tokens, tokens), 1)

    def as_column(row):
        return jnp.sum(jnp.where(diagonal, row, 0.0), axis=1, keepdims=True)

    rank_row = to_i32(rank_row)
    code_row = lax.div(owner_row, 16) * 256 + sent_place(owner_row) * TILE + rank_row
    none = -1

    utterance_col = to_i32(as_column(utterance_ref[...].reshape(1, tokens).astype(F32)))
    lane = iota((tokens, HD), 1)
    label_low = ones_where(lane == utterance_col)
    label_high = ones_where(lane == utterance_col + 64)

    def value_head(h):
        return value_ref[:, h * HD : (h + 1) * HD]

    def put(outgoing, block, lo, part):
        buffer, lent = outgoing
        width = part.shape[1]
        part = part.astype(BF16)
        out = pl.ds(block * 8, 8)
        buffer[out, my_c, :, lo : lo + width] = part[0:128].reshape(8, TILE, width)
        lent[out, :, lo : lo + width] = part[128:256].reshape(8, TILE, width)

    def pack_0(block, carry):
        span = pl.ds(pl.multiple_of(block * 256, 256), 256)
        row = iota((256, tokens), 0) + block * 256
        first = beside(
            ones_where(row == code_row),
            ones_where(row == jnp.where(rank_row < 4, code_row + 12, none)),
        )
        second = beside(
            ones_where(row == jnp.where(rank_row >= 4, code_row - 4, none)),
            ones_where(row == jnp.where(rank_row >= 4, code_row + 4, none)),
        )
        third = ones_where(row == jnp.where(rank_row < 8, code_row + 8, none))
        pack_first[span, :] = first
        pack_second[span, :] = second
        put(out_0, block, 0, mm(first, over(value_head(0), value_head(1))))
        put(out_0, block, HD, mm(second, over(value_head(1), label_high)) + mm(third, label_low))
        return carry

    lax.fori_loop(0, blocks, pack_0, 0)
    pl.semaphore_wait(barrier, chips - 1 + tensors - 1 + size_y)
    share(stat_norm, my_x, tensors, lambda to: {"tensor": to}, NORM)
    lend(out_0, OUT)

    code_col = to_i32(as_column(code_row_f))
    rank_col = code_col % TILE
    column = iota((tokens, rows), 1)
    unpack_first[...] = ones_where(column == code_col)
    unpack_low[...] = ones_where(column == jnp.where(rank_col < 4, code_col + 12, none))
    unpack_high_a[...] = ones_where(column == jnp.where(rank_col >= 4, code_col - 4, none))
    unpack_high_b[...] = ones_where(column == jnp.where(rank_col >= 4, code_col + 4, none))

    scatter(out_0, in_0, OUT)
    share_wait(stat_norm, tensors, NORM)
    total = stat_norm[0]
    for x in range(1, tensors):
        total = total + stat_norm[x]
    inverse = lax.rsqrt(total / feat_total + EPSILON)
    inverse_query_ref[...] = jnp.broadcast_to(inverse[:, 0:1], (tokens, HD))
    inverse_key_ref[...] = jnp.broadcast_to(inverse[:, 64:65], (tokens, HD))

    def gain_of(ref, h):
        return ref[h * HD : (h + 1) * HD].reshape(1, HD)

    def unit_query(h):
        return query_ref[:, h * HD : (h + 1) * HD].astype(F32) * inverse_query_ref[...]

    def unit_key(h):
        return key_ref[:, h * HD : (h + 1) * HD].astype(F32) * inverse_key_ref[...]

    def pack_qk(group, buffer, index):
        for h in (2 * group, 2 * group + 1):
            cols = slice(h * HD, (h + 1) * HD)
            normed[0:tokens, cols] = (gain_of(gain_query_ref, h) * unit_query(h)).astype(BF16)
            normed[tokens : 2 * tokens, cols] = (
                gain_of(gain_key_ref, h) * unit_key(h)
            ).astype(BF16)
        lo = group * 256

        def block_body(block, carry):
            span = pl.ds(pl.multiple_of(block * 256, 256), 256)
            first = pack_first[span, :]
            second = pack_second[span, :]
            keys = slice(tokens, 2 * tokens)
            put(buffer, block, 0, mm(first, normed[:, lo : lo + 256]))
            high = over(normed[keys, lo : lo + HD], normed[keys, lo + HD : lo + 256])
            put(buffer, block, 256, mm(second, high))
            if group == 1:
                v = [value_head(h) for h in range(HEADS)]
                put(buffer, block, 384, mm(first, over(beside(v[2], v[4]), beside(v[3], v[5]))))
                put(buffer, block, 640, mm(second, over(v[3], v[5])))
            return carry

        lax.fori_loop(0, blocks, block_body, 0)
        lend(buffer, index)

    pack_qk(0, out_1, OUT + 1)
    pack_qk(1, out_2, OUT + 2)
    scatter(out_1, in_1, OUT + 1)
    pack_qk(2, out_3, OUT + 3)
    settle(out_2, in_2, OUT + 2)
    send_part(out_2, in_2, OUT + 2, 0)

    def own_maps(own_axis, message_axis, shape, place_of):
        row = iota(shape, own_axis)
        message = iota(shape, message_axis)
        device = lax.div(row, SLOT)
        base = place_of(device) * TILE
        slot = row - device * SLOT
        first = ones_where(message == base + slot)
        low = ones_where((message == base + 12 + slot) & (slot < 4))
        high_a = ones_where((message == base + slot - 4) & (slot >= 4))
        high_b = ones_where((message == base + slot + 4) & (slot >= 4))
        labels = ones_where(message == base + 8 + slot - jnp.where(slot < 8, 0, 4))
        return first, low, high_a, high_b, labels

    first, low, high_a, high_b, label_map = own_maps(0, 1, (192, 256), lambda device: device)
    second_a = beside(low, high_a)
    second_b = beside(low, high_b)
    first_t, low_t, high_a_t, high_b_t, _ = own_maps(1, 0, (256, 192), sent_place)
    back_first = beside(first_t, low_t)
    back_second = beside(high_a_t, high_b_t)

    def message(buffer, src, tile):
        return buffer[src, :, tile * HD : (tile + 1) * HD].reshape(256, HD)

    wait_recv(in_0, OUT)

    def unpack_0(block, carry):
        span = pl.ds(pl.multiple_of(block * 192, 64), 192)
        src = pl.ds(block * 16, 16)
        t0 = message(in_0, src, 0)
        t1 = message(in_0, src, 1)
        value_own[0, span, :] = mm(first, t0).astype(BF16)
        value_own[1, span, :] = mm(second_a, over(t0, t1)).astype(BF16)
        found = mm(label_map, t1)
        early = iota((192, 1), 0) % SLOT < 8
        is_zero = jnp.where(early, found[:, 0:1], found[:, 64:65])
        is_one = jnp.where(early, found[:, 1:2], found[:, 65:66])
        spot = iota((192, HD), 1)
        member = jnp.where(
            spot == 0, is_zero, jnp.where(spot == 1, is_one, 1.0 - is_zero - is_one)
        )
        used = spot < 3
        extend_key[span, :] = jnp.where(used, member, 0.0).astype(BF16)
        extend_query[span, :] = jnp.where(used, FAR * (1.0 - member), 0.0).astype(BF16)
        return carry

    lax.fori_loop(0, blocks, unpack_0, 0)
    load_cotangent.wait()

    factor = HD**-0.5
    scale = factor * math.log2(math.e)
    chunk = 256 if own % 256 == 0 else own

    def attention_group(group, send_in_chunk):
        buffer = (in_1, in_2, in_3)[group]
        wait_recv(buffer, OUT + 1 + group)

        def unpack_body(block, carry):
            span = pl.ds(pl.multiple_of(block * 192, 64), 192)
            src = pl.ds(block * 16, 16)
            t0, t1, t2 = (message(buffer, src, i) for i in range(3))
            q = mm(first, beside(t0, t1)).astype(BF16)
            query_own[0, span, :] = q[:, 0:HD]
            query_own[1, span, :] = q[:, HD : 2 * HD]
            key_own[0, span, :] = mm(second_a, over(t0, t2)).astype(BF16)
            key_own[1, span, :] = mm(second_b, over(t1, t2)).astype(BF16)
            if group == 1:
                t0, t1, t2 = (message(buffer, src, i) for i in range(3, 6))
                v = mm(first, beside(t0, t1)).astype(BF16)
                value_own[2, span, :] = v[:, 0:HD]
                value_own[4, span, :] = v[:, HD : 2 * HD]
                value_own[3, span, :] = mm(second_a, over(t0, t2)).astype(BF16)
                value_own[5, span, :] = mm(second_b, over(t1, t2)).astype(BF16)
            return carry

        lax.fori_loop(0, blocks, unpack_body, 0)
        key_sum[...] = jnp.zeros((2, HD, own), F32)
        value_sum[...] = jnp.zeros((2, HD, own), F32)

        def row_body(index, carry):
            send_in_chunk(index)
            span = pl.ds(pl.multiple_of(index * chunk, chunk), chunk)
            for local in range(2):
                head = 2 * group + local
                cols = slice(head * HD, (head + 1) * HD)
                keys = key_own[local]
                values = value_own[head]
                q = query_own[local, span, :]
                cot = cotangent_ref[span, cols]
                scores = mm_nt(beside(q, extend_query[span, :]), beside(keys, extend_key[...]))
                raised = jnp.exp2((scores - jnp.max(scores, axis=1, keepdims=True)) * scale)
                weights = (raised * (1.0 / jnp.sum(raised, axis=1, keepdims=True))).astype(BF16)
                attended = mm(weights, values).astype(BF16)
                attended_ref[span, cols] = attended
                delta = jnp.sum(cot.astype(F32) * attended.astype(F32), axis=1, keepdims=True)
                grad_weights = mm_nt(cot, values)
                grad_scores = (weights.astype(F32) * (grad_weights - delta)).astype(BF16)
                grad_query_own[local, span, :] = (mm(grad_scores, keys) * factor).astype(BF16)
                value_sum[local] += mm(cot.T, weights)
                key_sum[local] += mm(q.T, grad_scores)
            return carry

        lax.fori_loop(0, own // chunk, row_body, 0)
        for local in range(2):
            grad_key_own[local] = (key_sum[local].T * factor).astype(BF16)
            grad_value_own[2 * group + local] = value_sum[local].T.astype(BF16)

        target = (back_0, back_1, back_2)[group]

        def pack_body(block, carry):
            span = pl.ds(pl.multiple_of(block * 192, 64), 192)
            q = beside(grad_query_own[0, span, :], grad_query_own[1, span, :])
            k = [grad_key_own[i, span, :] for i in range(2)]
            put(target, block, 0, mm(back_first, over(q, beside(k[0], k[1]))))
            put(target, block, 256, mm(back_second, over(k[0], k[1])))
            if group == 1:
                v = [grad_value_own[i, span, :] for i in range(4)]
                put(
                    target, block, 384, mm(back_first, over(beside(v[0], v[2]), beside(v[1], v[3])))
                )
                put(target, block, 640, mm(back_second, over(v[1], v[3])))
            return carry

        lax.fori_loop(0, blocks, pack_body, 0)
        lend(target, BACK + group)

    def send_later(outgoing, target, index):
        chunks = own // chunk

        def in_chunk(position):
            start = 1 + position * (size_y - 1) // chunks
            stop = 1 + (position + 1) * (size_y - 1) // chunks
            send_parts(outgoing, target, index, start, stop)

        return in_chunk

    attention_group(0, send_later(out_2, in_2, OUT + 2))
    settle(out_3, in_3, OUT + 3)
    send_part(out_3, in_3, OUT + 3, 0)
    settle(back_0, home_0, BACK)
    send_part(back_0, home_0, BACK, 0)
    rest_out = send_later(out_3, in_3, OUT + 3)
    rest_back = send_later(back_0, home_0, BACK)

    def both_rests(position):
        rest_out(position)
        rest_back(position)

    attention_group(1, both_rests)
    settle(back_1, home_1, BACK + 1)
    send_part(back_1, home_1, BACK + 1, 0)
    attention_group(2, send_later(back_1, home_1, BACK + 1))

    def pack_last(block, carry):
        span = pl.ds(pl.multiple_of(block * 192, 64), 192)
        v4 = grad_value_own[4, span, :]
        v5 = grad_value_own[5, span, :]
        put(back_3, block, 0, mm(back_first, over(v4, v5)))
        put(back_3, block, HD, mm(high_a_t, v5))
        return carry

    lax.fori_loop(0, blocks, pack_last, 0)
    lend(back_3, BACK + 3)
    scatter(back_2, home_2, BACK + 2)
    scatter(back_3, home_3, BACK + 3)
    save_attended = pltpu.make_async_copy(attended_ref, attended_hbm, local_sems.at[1])
    save_attended.start()

    near = my_y * size_c + my_c
    near_count = size_y * size_c
    center_query_ref[...] = jnp.zeros((tokens, HD), F32)
    center_key_ref[...] = jnp.zeros((tokens, HD), F32)
    gain_near[near] = jnp.zeros((16, HD), F32)

    def home_group(group):
        buffer = (home_0, home_1, home_2)[group]
        wait_recv(buffer, BACK + group)
        tile = lambda i: buffer[:, :, i * HD : (i + 1) * HD].reshape(rows, HD)
        both = beside(tile(0), tile(1))
        queries = mm(unpack_first[...], both)
        keys = mm(unpack_low[...], both)
        high = (mm(unpack_high_a[...], tile(2)), mm(unpack_high_b[...], tile(2)))
        for local in range(2):
            h = 2 * group + local
            cols = slice(h * HD, (h + 1) * HD)
            part = slice(local * HD, (local + 1) * HD)
            grad_q = queries[:, part].astype(BF16)
            grad_k = (keys[:, part] + high[local]).astype(BF16)
            grad_qn[:, cols] = grad_q
            grad_kn[:, cols] = grad_k
            term = grad_q.astype(F32) * unit_query(h)
            gain_near[near, h : h + 1, :] = jnp.sum(term, axis=0, keepdims=True)
            center_query_ref[...] += gain_of(gain_query_ref, h) * term
            term = grad_k.astype(F32) * unit_key(h)
            gain_near[near, 8 + h : 9 + h, :] = jnp.sum(term, axis=0, keepdims=True)
            center_key_ref[...] += gain_of(gain_key_ref, h) * term

    for group in range(3):
        home_group(group)

    stat_center[my_x] = jnp.where(
        half,
        jnp.sum(center_query_ref[...], axis=1, keepdims=True),
        jnp.sum(center_key_ref[...], axis=1, keepdims=True),
    )
    share(stat_center, my_x, tensors, lambda to: {"tensor": to}, CENTER)
    share(
        gain_near,
        near,
        near_count,
        lambda to: {"dp": ((to // size_c) * size_z + my_z) * size_c + to % size_c},
        NEAR,
    )

    def value_home(buffer, start, h):
        tile = lambda i: buffer[:, :, (start + i) * HD : (start + i + 1) * HD].reshape(rows, HD)
        both = beside(tile(0), tile(1))
        evens = mm(unpack_first[...], both)
        odds = mm(unpack_low[...], both)
        high = (mm(unpack_high_a[...], tile(2)), mm(unpack_high_b[...], tile(2)))
        for i in range(2):
            part = slice(i * HD, (i + 1) * HD)
            at = (h + 2 * i) * HD
            grad_value_ref[:, at : at + HD] = evens[:, part].astype(BF16)
            grad_value_ref[:, at + HD : at + 2 * HD] = (odds[:, part] + high[i]).astype(BF16)

    value_home(home_1, 3, 0)

    share_wait(gain_near, near_count, NEAR)
    total = gain_near[0]
    for i in range(1, near_count):
        total = total + gain_near[i]
    gain_far[my_z] = total
    share(
        gain_far,
        my_z,
        size_z,
        lambda to: {"dp": (my_y * size_z + to) * size_c + my_c},
        FARTHER,
    )

    share_wait(stat_center, tensors, CENTER)
    total = stat_center[0]
    for x in range(1, tensors):
        total = total + stat_center[x]
    total = total / feat_total
    center_q = jnp.broadcast_to(total[:, 0:1], (tokens, HD))
    center_k = jnp.broadcast_to(total[:, 64:65], (tokens, HD))
    for h in range(HEADS):
        cols = slice(h * HD, (h + 1) * HD)
        scaled = gain_of(gain_query_ref, h) * grad_qn[:, cols].astype(F32)
        grad_query_ref[:, cols] = (
            (scaled - unit_query(h) * center_q) * inverse_query_ref[...]
        ).astype(BF16)
        scaled = gain_of(gain_key_ref, h) * grad_kn[:, cols].astype(F32)
        grad_key_ref[:, cols] = (
            (scaled - unit_key(h) * center_k) * inverse_key_ref[...]
        ).astype(BF16)

    share_wait(gain_far, size_z, FARTHER)
    total = gain_far[0]
    for i in range(1, size_z):
        total = total + gain_far[i]
    for h in range(HEADS):
        gain_query_out[h * HD : (h + 1) * HD] = total[h : h + 1].reshape(HD)
        gain_key_out[h * HD : (h + 1) * HD] = total[8 + h : 9 + h].reshape(HD)

    wait_recv(home_3, BACK + 3)
    t0, t1 = (home_3[:, :, i * HD : (i + 1) * HD].reshape(rows, HD) for i in range(2))
    grad_value_ref[:, 4 * HD : 5 * HD] = mm(unpack_first[...], t0).astype(BF16)
    grad_value_ref[:, 5 * HD : 6 * HD] = (
        mm(unpack_low[...], t0) + mm(unpack_high_a[...], t1)
    ).astype(BF16)

    save_attended.wait()
    outgoing = (out_0, out_1, out_2, out_3, back_0, back_1, back_2, back_3)
    for i, (buffer, lent) in enumerate(outgoing):
        wait_send(buffer, OUT + i, chips - 1)
        wait_send(lent, LENT + i, chips)
    wait_send(stat_norm, NORM, tensors - 1)
    wait_send(stat_center, CENTER, tensors - 1)
    wait_send(gain_near, NEAR, near_count - 1)
    wait_send(gain_far, FARTHER, size_z - 1)


def copy_out(*refs):
    count = (len(refs) - 2) // 3
    sources, targets, held = (refs[i * count : (i + 1) * count] for i in range(3))
    load_sems, save_sems = refs[-2:]
    loads = [
        pltpu.make_async_copy(sources[i], held[i], load_sems.at[i]) for i in range(count)
    ]
    saves = [
        pltpu.make_async_copy(held[i], targets[i], save_sems.at[i]) for i in range(count)
    ]
    for load in loads:
        load.start()
    for load, save in zip(loads, saves):
        load.wait()
        save.start()
    for save in saves:
        save.wait()


def shards(query_raw, key_raw, value_rows, gain_query, gain_key, owner_id, utterance, cotangent):
    dp = lax.axis_size("dp")
    tensors = lax.axis_size("tensor")
    tokens, feat = query_raw.shape
    rows = dp * TILE
    own = dp * SLOT
    _, size_z, _ = SHAPES[dp]
    vmem = pl.BlockSpec(memory_space=pltpu.VMEM)
    anywhere = pl.BlockSpec(memory_space=pl.ANY)
    out_shape = (
        jax.ShapeDtypeStruct((own, feat), BF16),
        jax.ShapeDtypeStruct((tokens, feat), BF16),
        jax.ShapeDtypeStruct((tokens, feat), BF16),
        jax.ShapeDtypeStruct((tokens, feat), BF16),
        jax.ShapeDtypeStruct((feat,), F32),
        jax.ShapeDtypeStruct((feat,), F32),
    )
    chips = dp // 2

    def outgoing(*widths):
        shapes = [
            shape for w in widths for shape in ((chips, 2, TILE, w), (chips, TILE, w))
        ]
        return [pltpu.VMEM(shape, BF16) for shape in shapes]

    def incoming(*widths):
        return [pltpu.VMEM((dp, TILE, width), BF16) for width in widths]

    scratch = (
        [
            pltpu.VMEM((rows, 2 * tokens), BF16),
            pltpu.VMEM((rows, 2 * tokens), BF16),
            pltpu.VMEM((tokens, rows), BF16),
            pltpu.VMEM((tokens, rows), BF16),
            pltpu.VMEM((tokens, rows), BF16),
            pltpu.VMEM((tokens, rows), BF16),
            pltpu.VMEM((2 * tokens, feat), BF16),
            pltpu.VMEM((tokens, HD), F32),
            pltpu.VMEM((tokens, HD), F32),
        ]
        + outgoing(256, 384, 768, 384)
        + incoming(256, 384, 768, 384)
        + outgoing(384, 768, 384, 256)
        + incoming(384, 768, 384, 256)
        + [
            pltpu.VMEM((HEADS, own, HD), BF16),
            pltpu.VMEM((HEADS, own, HD), BF16),
            pltpu.VMEM((own, HD), BF16),
            pltpu.VMEM((own, HD), BF16),
            pltpu.VMEM((2, own, HD), BF16),
            pltpu.VMEM((2, own, HD), BF16),
            pltpu.VMEM((2, own, HD), BF16),
            pltpu.VMEM((2, own, HD), BF16),
            pltpu.VMEM((2, HD, own), F32),
            pltpu.VMEM((2, HD, own), F32),
            pltpu.VMEM((tokens, feat), BF16),
            pltpu.VMEM((tokens, feat), BF16),
            pltpu.VMEM((tokens, HD), F32),
            pltpu.VMEM((tokens, HD), F32),
            pltpu.VMEM((tensors, tokens, HD), F32),
            pltpu.VMEM((tensors, tokens, HD), F32),
            pltpu.VMEM((dp // size_z, 16, HD), F32),
            pltpu.VMEM((size_z, 16, HD), F32),
            pltpu.VMEM((own, feat), BF16),
            pltpu.VMEM((own, feat), BF16),
            pltpu.SemaphoreType.DMA((20,)),
            pltpu.SemaphoreType.DMA((20,)),
            pltpu.SemaphoreType.DMA((2,)),
        ]
    )
    results = pl.pallas_call(
        functools.partial(kernel, dp, tensors, tokens),
        out_shape=out_shape,
        in_specs=[vmem] * 7 + [anywhere],
        out_specs=[anywhere] + [vmem] * 5,
        scratch_shapes=scratch,
        compiler_params=pltpu.CompilerParams(
            collective_id=0, has_side_effects=True, vmem_limit_bytes=58 * 1024 * 1024
        ),
    )(
        query_raw,
        key_raw,
        value_rows,
        gain_query,
        gain_key,
        owner_id,
        utterance,
        cotangent,
    )
    return pl.pallas_call(
        copy_out,
        out_shape=out_shape,
        in_specs=[anywhere] * 6,
        out_specs=[anywhere] * 6,
        scratch_shapes=[pltpu.VMEM(out.shape, out.dtype) for out in out_shape]
        + [pltpu.SemaphoreType.DMA((6,)), pltpu.SemaphoreType.DMA((6,))],
        compiler_params=pltpu.CompilerParams(vmem_limit_bytes=58 * 1024 * 1024),
    )(*results)


def solution(mesh):
    wide = P("dp", "tensor")
    return jax.shard_map(
        shards,
        mesh=mesh,
        in_specs=(wide, wide, wide, P("tensor"), P("tensor"), P("dp"), P("dp"), wide),
        out_specs=(wide, wide, wide, wide, P("tensor"), P("tensor")),
        check_vma=False,
    )
```

```python
import functools
import math

import jax
import jax.numpy as jnp
from jax import lax
from jax.experimental import pallas as pl
from jax.experimental.pallas import tpu as pltpu
from jax.sharding import PartitionSpec as P

HD = 128
EPSILON = 1e-06
SLOT = 12
TILE = 16
HEADS = 6
GROUPS = 3
PART = 32
FAR = -(2.0**30)
F32 = jnp.float32
BF16 = jnp.bfloat16
MESH = pl.DeviceIdType.MESH
ORDER = {8: (3, -1, 2, -2, 0, -3, 1, 4), 4: (-1, 1, 0, 2)}
SHAPES = {64: (4, 8, 2), 16: (2, 4, 2)}


def mm(a, b):
    return lax.dot_general(a, b, (((1,), (0,)), ((), ())), preferred_element_type=F32)


def mm_nt(a, b):
    return lax.dot_general(a, b, (((1,), (1,)), ((), ())), preferred_element_type=F32)


def iota(shape, axis):
    return lax.broadcasted_iota(jnp.int32, shape, axis)


def ones_where(mask):
    return jnp.where(mask, 1.0, 0.0).astype(BF16)


def to_i32(x):
    return x.astype(jnp.int32)


def over(*parts):
    return jnp.concatenate(parts, axis=0)


def beside(*parts):
    return jnp.concatenate(parts, axis=1)


def kernel(
    dp,
    tensors,
    tokens,
    query_ref,
    key_ref,
    value_ref,
    gain_query_ref,
    gain_key_ref,
    owner_ref,
    utterance_ref,
    cotangent_hbm,
    attended_hbm,
    grad_query_hbm,
    grad_key_hbm,
    grad_value_ref,
    gain_query_out,
    gain_key_out,
    pack_first,
    pack_second,
    unpack_first,
    unpack_low,
    unpack_high_a,
    unpack_high_b,
    normed,
    inverse_query_ref,
    inverse_key_ref,
    out_0,
    out_0_lent,
    out_1,
    out_1_lent,
    out_2,
    out_2_lent,
    out_3,
    out_3_lent,
    in_0,
    in_1,
    in_2,
    in_3,
    back_0,
    back_0_lent,
    back_1,
    back_1_lent,
    back_2,
    back_2_lent,
    back_3,
    back_3_lent,
    home_0,
    home_1,
    home_2,
    home_3,
    value_own,
    grad_value_own,
    extend_query,
    extend_key,
    query_own,
    key_own,
    grad_query_own,
    grad_key_own,
    key_sum,
    value_sum,
    grad_qn,
    grad_kn,
    center_query_ref,
    center_key_ref,
    stat_norm,
    stat_center,
    gain_near,
    gain_far,
    cotangent_ref,
    attended_ref,
    grad_query_ref,
    grad_key_ref,
    send_sems,
    recv_sems,
    local_sems,
):
    size_y, size_z, size_c = SHAPES[dp]
    me = lax.axis_index("dp")
    my_x = lax.axis_index("tensor")
    my_c = me % size_c
    my_z = (me // size_c) % size_z
    my_y = me // (size_c * size_z)
    rows = dp * TILE
    own = dp * SLOT
    feat = HEADS * HD
    feat_total = feat * tensors
    blocks = dp // 16

    chips = size_y * size_z
    my_chip = my_y * size_z + my_z
    way = 1 - 2 * my_c
    z_of = {step: lax.rem(my_z + way * step + size_z, size_z) for step in ORDER[size_z]}
    y_of = [lax.rem(my_y + step, size_y) for step in range(size_y)]

    def put_to(source, target, send_index, recv_index, chip, core):
        pltpu.make_async_remote_copy(
            src_ref=source,
            dst_ref=target,
            send_sem=send_sems.at[send_index],
            recv_sem=recv_sems.at[recv_index],
            device_id={"dp": chip * size_c + core},
            device_id_type=MESH,
        ).start()

    def lend(outgoing, index):
        buffer, lent = outgoing
        put_to(lent, buffer.at[:, my_c], LENT + index, LENT + index, my_chip, 1 - my_c)

    def pair_of(target, chip):
        return target.at[pl.ds(chip * size_c, size_c)]

    def settle(outgoing, target, index):
        buffer, lent = outgoing
        pltpu.make_async_copy(lent, lent, recv_sems.at[LENT + index]).wait()
        pltpu.make_async_copy(
            buffer.at[my_chip], pair_of(target, my_chip), recv_sems.at[index]
        ).start()

    def send_part(outgoing, target, index, step):
        buffer, _ = outgoing
        for place, step_z in enumerate(ORDER[size_z]):
            chip = lax.rem(my_y + step + place, size_y) * size_z + z_of[step_z]

            def send(chip=chip):
                put_to(buffer.at[chip], pair_of(target, my_chip), index, index, chip, my_c)

            if step_z == 0:
                pl.when(step > 0)(send)
            else:
                send()

    def send_parts(outgoing, target, index, start, stop):
        def body(step, carry):
            send_part(outgoing, target, index, step)
            return carry

        lax.fori_loop(start, stop, body, 0)

    def scatter(outgoing, target, index):
        settle(outgoing, target, index)
        send_parts(outgoing, target, index, 0, size_y)

    def wait_recv(target, index):
        pltpu.make_async_copy(target, target, recv_sems.at[index]).wait()

    def wait_send(source, index, count):
        part = source.at[pl.ds(0, count)]
        pltpu.make_async_copy(part, part, send_sems.at[index]).wait()

    def share(buffer, slot, count, device_of, index):
        def step_body(step, carry):
            to = lax.rem(slot + step, count)
            pltpu.make_async_remote_copy(
                src_ref=buffer.at[slot],
                dst_ref=buffer.at[slot],
                send_sem=send_sems.at[index],
                recv_sem=recv_sems.at[index],
                device_id=device_of(to),
                device_id_type=MESH,
            ).start()
            return carry

        lax.fori_loop(1, count, step_body, 0)

    def share_wait(buffer, count, index):
        part = buffer.at[pl.ds(0, count - 1)]
        pltpu.make_async_copy(part, part, recv_sems.at[index]).wait()

    OUT, BACK, LENT, NORM, CENTER, NEAR, FARTHER = 0, 4, 8, 16, 17, 18, 19

    barrier = pltpu.get_barrier_semaphore()

    def greet(device_id):
        pl.semaphore_signal(barrier, inc=1, device_id=device_id, device_id_type=MESH)

    def greet_chip(step, carry):
        greet({"dp": lax.rem(me + step * size_c, dp)})
        return carry

    for step in range(1, tensors):
        greet({"tensor": lax.rem(my_x + step, tensors)})
    for step in range(size_y):
        greet({"dp": (y_of[step] * size_z + my_z) * size_c + 1 - my_c})
    lax.fori_loop(1, chips, greet_chip, 0)
    load_cotangent = pltpu.make_async_copy(cotangent_hbm, cotangent_ref, local_sems.at[0])
    load_cotangent.start()

    out_0, out_1, out_2, out_3 = zip(
        (out_0, out_1, out_2, out_3), (out_0_lent, out_1_lent, out_2_lent, out_3_lent)
    )
    back_0, back_1, back_2, back_3 = zip(
        (back_0, back_1, back_2, back_3), (back_0_lent, back_1_lent, back_2_lent, back_3_lent)
    )

    owner_row = owner_ref[...].reshape(1, tokens)
    chosen = jnp.where(iota((dp, tokens), 0) == owner_row, 1.0, 0.0)
    upper = ones_where(iota((tokens, tokens), 0) < iota((tokens, tokens), 1))
    rank_row = jnp.sum(mm(chosen.astype(BF16), upper) * chosen, axis=0, keepdims=True)
    code_row_f = owner_row.astype(F32) * TILE + rank_row

    def sent_place(peer):
        return lax.rem(peer + my_c, 2) * 8 + lax.div(lax.rem(peer, 16), 2)

    diagonal = iota((tokens, tokens), 0) == iota((tokens, tokens), 1)

    def as_column(row):
        return jnp.sum(jnp.where(diagonal, row, 0.0), axis=1, keepdims=True)

    rank_row = to_i32(rank_row)
    code_row = lax.div(owner_row, 16) * 256 + sent_place(owner_row) * TILE + rank_row
    none = -1

    utterance_col = to_i32(as_column(utterance_ref[...].reshape(1, tokens).astype(F32)))
    lane = iota((tokens, HD), 1)
    label_low = ones_where(lane == utterance_col)
    label_high = ones_where(lane == utterance_col + 64)

    def value_head(h):
        return value_ref[:, h * HD : (h + 1) * HD]

    def put(outgoing, block, lo, part):
        buffer, lent = outgoing
        width = part.shape[1]
        part = part.astype(BF16)
        out = pl.ds(block * 8, 8)
        buffer[out, my_c, :, lo : lo + width] = part[0:128].reshape(8, TILE, width)
        lent[out, :, lo : lo + width] = part[128:256].reshape(8, TILE, width)

    def pack_0(block, carry):
        span = pl.ds(pl.multiple_of(block * 256, 256), 256)
        row = iota((256, tokens), 0) + block * 256
        first = beside(
            ones_where(row == code_row),
            ones_where(row == jnp.where(rank_row < 4, code_row + 12, none)),
        )
        second = beside(
            ones_where(row == jnp.where(rank_row >= 4, code_row - 4, none)),
            ones_where(row == jnp.where(rank_row >= 4, code_row + 4, none)),
        )
        third = ones_where(row == jnp.where(rank_row < 8, code_row + 8, none))
        pack_first[span, :] = first
        pack_second[span, :] = second
        put(out_0, block, 0, mm(first, over(value_head(0), value_head(1))))
        put(out_0, block, HD, mm(second, over(value_head(1), label_high)) + mm(third, label_low))
        return carry

    lax.fori_loop(0, blocks, pack_0, 0)
    pl.semaphore_wait(barrier, chips - 1 + tensors - 1 + size_y)
    lend(out_0, OUT)

    half = iota((tokens, HD), 1) < 64
    query_f = query_ref[...].astype(F32)
    key_f = key_ref[...].astype(F32)
    stat_norm[my_x] = jnp.where(
        half,
        jnp.sum(query_f * query_f, axis=1, keepdims=True),
        jnp.sum(key_f * key_f, axis=1, keepdims=True),
    )
    share(stat_norm, my_x, tensors, lambda to: {"tensor": to}, NORM)
    scatter(out_0, in_0, OUT)


    code_col = to_i32(as_column(code_row_f))
    rank_col = code_col % TILE
    column = iota((tokens, rows), 1)
    unpack_first[...] = ones_where(column == code_col)
    unpack_low[...] = ones_where(column == jnp.where(rank_col < 4, code_col + 12, none))
    unpack_high_a[...] = ones_where(column == jnp.where(rank_col >= 4, code_col - 4, none))
    unpack_high_b[...] = ones_where(column == jnp.where(rank_col >= 4, code_col + 4, none))

    share_wait(stat_norm, tensors, NORM)
    total = stat_norm[0]
    for x in range(1, tensors):
        total = total + stat_norm[x]
    inverse = lax.rsqrt(total / feat_total + EPSILON)
    inverse_query_ref[...] = jnp.broadcast_to(inverse[:, 0:1], (tokens, HD))
    inverse_key_ref[...] = jnp.broadcast_to(inverse[:, 64:65], (tokens, HD))

    def gain_of(ref, h):
        return ref[h * HD : (h + 1) * HD].reshape(1, HD)

    def unit_query(h):
        return query_ref[:, h * HD : (h + 1) * HD].astype(F32) * inverse_query_ref[...]

    def unit_key(h):
        return key_ref[:, h * HD : (h + 1) * HD].astype(F32) * inverse_key_ref[...]

    def pack_qk(group, buffer, index):
        for h in (2 * group, 2 * group + 1):
            cols = slice(h * HD, (h + 1) * HD)
            normed[0:tokens, cols] = (gain_of(gain_query_ref, h) * unit_query(h)).astype(BF16)
            normed[tokens : 2 * tokens, cols] = (
                gain_of(gain_key_ref, h) * unit_key(h)
            ).astype(BF16)
        lo = group * 256

        def block_body(block, carry):
            span = pl.ds(pl.multiple_of(block * 256, 256), 256)
            first = pack_first[span, :]
            second = pack_second[span, :]
            keys = slice(tokens, 2 * tokens)
            put(buffer, block, 0, mm(first, normed[:, lo : lo + 256]))
            high = over(normed[keys, lo : lo + HD], normed[keys, lo + HD : lo + 256])
            put(buffer, block, 256, mm(second, high))
            if group == 1:
                v = [value_head(h) for h in range(HEADS)]
                put(buffer, block, 384, mm(first, over(beside(v[2], v[4]), beside(v[3], v[5]))))
                put(buffer, block, 640, mm(second, over(v[3], v[5])))
            return carry

        lax.fori_loop(0, blocks, block_body, 0)
        lend(buffer, index)

    pack_qk(0, out_1, OUT + 1)
    pack_qk(1, out_2, OUT + 2)
    scatter(out_1, in_1, OUT + 1)
    pack_qk(2, out_3, OUT + 3)
    settle(out_2, in_2, OUT + 2)
    send_part(out_2, in_2, OUT + 2, 0)

    def own_maps(own_axis, message_axis, shape, place_of):
        row = iota(shape, own_axis)
        message = iota(shape, message_axis)
        device = lax.div(row, SLOT)
        base = place_of(device) * TILE
        slot = row - device * SLOT
        first = ones_where(message == base + slot)
        low = ones_where((message == base + 12 + slot) & (slot < 4))
        high_a = ones_where((message == base + slot - 4) & (slot >= 4))
        high_b = ones_where((message == base + slot + 4) & (slot >= 4))
        labels = ones_where(message == base + 8 + slot - jnp.where(slot < 8, 0, 4))
        return first, low, high_a, high_b, labels

    first, low, high_a, high_b, label_map = own_maps(0, 1, (192, 256), lambda device: device)
    second_a = beside(low, high_a)
    second_b = beside(low, high_b)
    first_t, low_t, high_a_t, high_b_t, _ = own_maps(1, 0, (256, 192), sent_place)
    back_first = beside(first_t, low_t)
    back_second = beside(high_a_t, high_b_t)

    def message(buffer, src, tile):
        return buffer[src, :, tile * HD : (tile + 1) * HD].reshape(256, HD)

    wait_recv(in_0, OUT)

    def unpack_0(block, carry):
        span = pl.ds(pl.multiple_of(block * 192, 64), 192)
        src = pl.ds(block * 16, 16)
        t0 = message(in_0, src, 0)
        t1 = message(in_0, src, 1)
        value_own[0, span, :] = mm(first, t0).astype(BF16)
        value_own[1, span, :] = mm(second_a, over(t0, t1)).astype(BF16)
        found = mm(label_map, t1)
        early = iota((192, 1), 0) % SLOT < 8
        is_zero = jnp.where(early, found[:, 0:1], found[:, 64:65])
        is_one = jnp.where(early, found[:, 1:2], found[:, 65:66])
        spot = iota((192, HD), 1)
        member = jnp.where(
            spot == 0, is_zero, jnp.where(spot == 1, is_one, 1.0 - is_zero - is_one)
        )
        used = spot < 3
        extend_key[span, :] = jnp.where(used, member, 0.0).astype(BF16)
        extend_query[span, :] = jnp.where(used, FAR * (1.0 - member), 0.0).astype(BF16)
        return carry

    lax.fori_loop(0, blocks, unpack_0, 0)
    load_cotangent.wait()

    factor = HD**-0.5
    scale = factor * math.log2(math.e)
    chunk = 256 if own % 256 == 0 else own

    def softmax(scores):
        raised = jnp.exp2((scores - jnp.max(scores, axis=1, keepdims=True)) * scale)
        return (raised * (1.0 / jnp.sum(raised, axis=1, keepdims=True))).astype(BF16)

    def attention_group(group, send_in_chunk):
        buffer = (in_1, in_2, in_3)[group]
        wait_recv(buffer, OUT + 1 + group)

        def unpack_body(block, carry):
            span = pl.ds(pl.multiple_of(block * 192, 64), 192)
            src = pl.ds(block * 16, 16)
            t0, t1, t2 = (message(buffer, src, i) for i in range(3))
            q = mm(first, beside(t0, t1)).astype(BF16)
            query_own[0, span, :] = q[:, 0:HD]
            query_own[1, span, :] = q[:, HD : 2 * HD]
            key_own[0, span, :] = mm(second_a, over(t0, t2)).astype(BF16)
            key_own[1, span, :] = mm(second_b, over(t1, t2)).astype(BF16)
            if group == 1:
                t0, t1, t2 = (message(buffer, src, i) for i in range(3, 6))
                v = mm(first, beside(t0, t1)).astype(BF16)
                value_own[2, span, :] = v[:, 0:HD]
                value_own[4, span, :] = v[:, HD : 2 * HD]
                value_own[3, span, :] = mm(second_a, over(t0, t2)).astype(BF16)
                value_own[5, span, :] = mm(second_b, over(t1, t2)).astype(BF16)
            return carry

        lax.fori_loop(0, blocks, unpack_body, 0)
        key_sum[...] = jnp.zeros((2, HD, own), F32)
        value_sum[...] = jnp.zeros((2, HD, own), F32)

        def row_body(index, carry):
            send_in_chunk(index)
            span = pl.ds(pl.multiple_of(index * chunk, chunk), chunk)
            for local in range(2):
                head = 2 * group + local
                cols = slice(head * HD, (head + 1) * HD)
                keys = key_own[local]
                values = value_own[head]
                q = query_own[local, span, :]
                cot = cotangent_ref[span, cols]
                scores = mm_nt(beside(q, extend_query[span, :]), beside(keys, extend_key[...]))
                weights = over(*(softmax(scores[r : r + PART]) for r in range(0, chunk, PART)))
                attended = mm(weights, values).astype(BF16)
                attended_ref[span, cols] = attended
                delta = jnp.sum(cot.astype(F32) * attended.astype(F32), axis=1, keepdims=True)
                grad_weights = mm_nt(cot, values)
                grad_scores = over(
                    *(
                        (
                            weights[r : r + PART].astype(F32)
                            * (grad_weights[r : r + PART] - delta[r : r + PART])
                        ).astype(BF16)
                        for r in range(0, chunk, PART)
                    )
                )
                grad_query_own[local, span, :] = (mm(grad_scores, keys) * factor).astype(BF16)
                value_sum[local] += mm(cot.T, weights)
                key_sum[local] += mm(q.T, grad_scores)
            return carry

        lax.fori_loop(0, own // chunk, row_body, 0)
        for local in range(2):
            grad_key_own[local] = (key_sum[local].T * factor).astype(BF16)
            grad_value_own[2 * group + local] = value_sum[local].T.astype(BF16)

        target = (back_0, back_1, back_2)[group]

        def pack_body(block, carry):
            span = pl.ds(pl.multiple_of(block * 192, 64), 192)
            q = beside(grad_query_own[0, span, :], grad_query_own[1, span, :])
            k = [grad_key_own[i, span, :] for i in range(2)]
            put(target, block, 0, mm(back_first, over(q, beside(k[0], k[1]))))
            put(target, block, 256, mm(back_second, over(k[0], k[1])))
            if group == 1:
                v = [grad_value_own[i, span, :] for i in range(4)]
                put(
                    target, block, 384, mm(back_first, over(beside(v[0], v[2]), beside(v[1], v[3])))
                )
                put(target, block, 640, mm(back_second, over(v[1], v[3])))
            return carry

        lax.fori_loop(0, blocks, pack_body, 0)
        lend(target, BACK + group)

    def send_later(outgoing, target, index):
        chunks = own // chunk

        def in_chunk(position):
            start = 1 + position * (size_y - 1) // chunks
            stop = 1 + (position + 1) * (size_y - 1) // chunks
            send_parts(outgoing, target, index, start, stop)

        return in_chunk

    attention_group(0, send_later(out_2, in_2, OUT + 2))
    settle(out_3, in_3, OUT + 3)
    send_part(out_3, in_3, OUT + 3, 0)
    settle(back_0, home_0, BACK)
    send_part(back_0, home_0, BACK, 0)
    rest_out = send_later(out_3, in_3, OUT + 3)
    rest_back = send_later(back_0, home_0, BACK)

    def both_rests(position):
        rest_out(position)
        rest_back(position)

    attention_group(1, both_rests)
    settle(back_1, home_1, BACK + 1)
    send_part(back_1, home_1, BACK + 1, 0)
    attention_group(2, send_later(back_1, home_1, BACK + 1))

    def pack_last(block, carry):
        span = pl.ds(pl.multiple_of(block * 192, 64), 192)
        v4 = grad_value_own[4, span, :]
        v5 = grad_value_own[5, span, :]
        put(back_3, block, 0, mm(back_first, over(v4, v5)))
        put(back_3, block, HD, mm(high_a_t, v5))
        return carry

    lax.fori_loop(0, blocks, pack_last, 0)
    lend(back_3, BACK + 3)
    scatter(back_2, home_2, BACK + 2)
    scatter(back_3, home_3, BACK + 3)
    save_attended = pltpu.make_async_copy(attended_ref, attended_hbm, local_sems.at[1])
    save_attended.start()

    near = my_y * size_c + my_c
    near_count = size_y * size_c
    center_query_ref[...] = jnp.zeros((tokens, HD), F32)
    center_key_ref[...] = jnp.zeros((tokens, HD), F32)
    gain_near[near] = jnp.zeros((16, HD), F32)

    def home_group(group):
        buffer = (home_0, home_1, home_2)[group]
        wait_recv(buffer, BACK + group)
        tile = lambda i: buffer[:, :, i * HD : (i + 1) * HD].reshape(rows, HD)
        both = beside(tile(0), tile(1))
        queries = mm(unpack_first[...], both)
        keys = mm(unpack_low[...], both)
        high = (mm(unpack_high_a[...], tile(2)), mm(unpack_high_b[...], tile(2)))
        for local in range(2):
            h = 2 * group + local
            cols = slice(h * HD, (h + 1) * HD)
            part = slice(local * HD, (local + 1) * HD)
            grad_q = queries[:, part].astype(BF16)
            grad_k = (keys[:, part] + high[local]).astype(BF16)
            grad_qn[:, cols] = grad_q
            grad_kn[:, cols] = grad_k
            term = grad_q.astype(F32) * unit_query(h)
            gain_near[near, h : h + 1, :] = jnp.sum(term, axis=0, keepdims=True)
            center_query_ref[...] += gain_of(gain_query_ref, h) * term
            term = grad_k.astype(F32) * unit_key(h)
            gain_near[near, 8 + h : 9 + h, :] = jnp.sum(term, axis=0, keepdims=True)
            center_key_ref[...] += gain_of(gain_key_ref, h) * term

    for group in range(3):
        home_group(group)

    stat_center[my_x] = jnp.where(
        half,
        jnp.sum(center_query_ref[...], axis=1, keepdims=True),
        jnp.sum(center_key_ref[...], axis=1, keepdims=True),
    )
    share(stat_center, my_x, tensors, lambda to: {"tensor": to}, CENTER)
    share(
        gain_near,
        near,
        near_count,
        lambda to: {"dp": ((to // size_c) * size_z + my_z) * size_c + to % size_c},
        NEAR,
    )

    def value_home(buffer, start, h):
        tile = lambda i: buffer[:, :, (start + i) * HD : (start + i + 1) * HD].reshape(rows, HD)
        both = beside(tile(0), tile(1))
        evens = mm(unpack_first[...], both)
        odds = mm(unpack_low[...], both)
        high = (mm(unpack_high_a[...], tile(2)), mm(unpack_high_b[...], tile(2)))
        for i in range(2):
            part = slice(i * HD, (i + 1) * HD)
            at = (h + 2 * i) * HD
            grad_value_ref[:, at : at + HD] = evens[:, part].astype(BF16)
            grad_value_ref[:, at + HD : at + 2 * HD] = (odds[:, part] + high[i]).astype(BF16)

    value_home(home_1, 3, 0)

    share_wait(gain_near, near_count, NEAR)
    total = gain_near[0]
    for i in range(1, near_count):
        total = total + gain_near[i]
    gain_far[my_z] = total
    share(
        gain_far,
        my_z,
        size_z,
        lambda to: {"dp": (my_y * size_z + to) * size_c + my_c},
        FARTHER,
    )

    share_wait(stat_center, tensors, CENTER)
    total = stat_center[0]
    for x in range(1, tensors):
        total = total + stat_center[x]
    total = total / feat_total
    center_q = jnp.broadcast_to(total[:, 0:1], (tokens, HD))
    center_k = jnp.broadcast_to(total[:, 64:65], (tokens, HD))
    for h in range(HEADS):
        cols = slice(h * HD, (h + 1) * HD)
        scaled = gain_of(gain_query_ref, h) * grad_qn[:, cols].astype(F32)
        grad_query_ref[:, cols] = (
            (scaled - unit_query(h) * center_q) * inverse_query_ref[...]
        ).astype(BF16)
        scaled = gain_of(gain_key_ref, h) * grad_kn[:, cols].astype(F32)
        grad_key_ref[:, cols] = (
            (scaled - unit_key(h) * center_k) * inverse_key_ref[...]
        ).astype(BF16)

    save_query = pltpu.make_async_copy(grad_query_ref, grad_query_hbm, local_sems.at[2])
    save_key = pltpu.make_async_copy(grad_key_ref, grad_key_hbm, local_sems.at[3])
    save_query.start()
    save_key.start()

    share_wait(gain_far, size_z, FARTHER)
    total = gain_far[0]
    for i in range(1, size_z):
        total = total + gain_far[i]
    for h in range(HEADS):
        gain_query_out[h * HD : (h + 1) * HD] = total[h : h + 1].reshape(HD)
        gain_key_out[h * HD : (h + 1) * HD] = total[8 + h : 9 + h].reshape(HD)

    wait_recv(home_3, BACK + 3)
    t0, t1 = (home_3[:, :, i * HD : (i + 1) * HD].reshape(rows, HD) for i in range(2))
    grad_value_ref[:, 4 * HD : 5 * HD] = mm(unpack_first[...], t0).astype(BF16)
    grad_value_ref[:, 5 * HD : 6 * HD] = (
        mm(unpack_low[...], t0) + mm(unpack_high_a[...], t1)
    ).astype(BF16)

    save_attended.wait()
    save_query.wait()
    save_key.wait()
    outgoing = (out_0, out_1, out_2, out_3, back_0, back_1, back_2, back_3)
    for i, (buffer, lent) in enumerate(outgoing):
        wait_send(buffer, OUT + i, chips - 1)
        wait_send(lent, LENT + i, chips)
    wait_send(stat_norm, NORM, tensors - 1)
    wait_send(stat_center, CENTER, tensors - 1)
    wait_send(gain_near, NEAR, near_count - 1)
    wait_send(gain_far, FARTHER, size_z - 1)


def copy_out(*refs):
    count = (len(refs) - 2) // 3
    sources, targets, held = (refs[i * count : (i + 1) * count] for i in range(3))
    load_sems, save_sems = refs[-2:]
    loads = [
        pltpu.make_async_copy(sources[i], held[i], load_sems.at[i]) for i in range(count)
    ]
    saves = [
        pltpu.make_async_copy(held[i], targets[i], save_sems.at[i]) for i in range(count)
    ]
    for load in loads:
        load.start()
    for load, save in zip(loads, saves):
        load.wait()
        save.start()
    for save in saves:
        save.wait()


def shards(query_raw, key_raw, value_rows, gain_query, gain_key, owner_id, utterance, cotangent):
    dp = lax.axis_size("dp")
    tensors = lax.axis_size("tensor")
    tokens, feat = query_raw.shape
    rows = dp * TILE
    own = dp * SLOT
    _, size_z, _ = SHAPES[dp]
    vmem = pl.BlockSpec(memory_space=pltpu.VMEM)
    anywhere = pl.BlockSpec(memory_space=pl.ANY)
    out_shape = (
        jax.ShapeDtypeStruct((own, feat), BF16),
        jax.ShapeDtypeStruct((tokens, feat), BF16),
        jax.ShapeDtypeStruct((tokens, feat), BF16),
        jax.ShapeDtypeStruct((tokens, feat), BF16),
        jax.ShapeDtypeStruct((feat,), F32),
        jax.ShapeDtypeStruct((feat,), F32),
    )
    chips = dp // 2

    def outgoing(*widths):
        shapes = [
            shape for w in widths for shape in ((chips, 2, TILE, w), (chips, TILE, w))
        ]
        return [pltpu.VMEM(shape, BF16) for shape in shapes]

    def incoming(*widths):
        return [pltpu.VMEM((dp, TILE, width), BF16) for width in widths]

    scratch = (
        [
            pltpu.VMEM((rows, 2 * tokens), BF16),
            pltpu.VMEM((rows, 2 * tokens), BF16),
            pltpu.VMEM((tokens, rows), BF16),
            pltpu.VMEM((tokens, rows), BF16),
            pltpu.VMEM((tokens, rows), BF16),
            pltpu.VMEM((tokens, rows), BF16),
            pltpu.VMEM((2 * tokens, feat), BF16),
            pltpu.VMEM((tokens, HD), F32),
            pltpu.VMEM((tokens, HD), F32),
        ]
        + outgoing(256, 384, 768, 384)
        + incoming(256, 384, 768, 384)
        + outgoing(384, 768, 384, 256)
        + incoming(384, 768, 384, 256)
        + [
            pltpu.VMEM((HEADS, own, HD), BF16),
            pltpu.VMEM((HEADS, own, HD), BF16),
            pltpu.VMEM((own, HD), BF16),
            pltpu.VMEM((own, HD), BF16),
            pltpu.VMEM((2, own, HD), BF16),
            pltpu.VMEM((2, own, HD), BF16),
            pltpu.VMEM((2, own, HD), BF16),
            pltpu.VMEM((2, own, HD), BF16),
            pltpu.VMEM((2, HD, own), F32),
            pltpu.VMEM((2, HD, own), F32),
            pltpu.VMEM((tokens, feat), BF16),
            pltpu.VMEM((tokens, feat), BF16),
            pltpu.VMEM((tokens, HD), F32),
            pltpu.VMEM((tokens, HD), F32),
            pltpu.VMEM((tensors, tokens, HD), F32),
            pltpu.VMEM((tensors, tokens, HD), F32),
            pltpu.VMEM((dp // size_z, 16, HD), F32),
            pltpu.VMEM((size_z, 16, HD), F32),
            pltpu.VMEM((own, feat), BF16),
            pltpu.VMEM((own, feat), BF16),
            pltpu.VMEM((tokens, feat), BF16),
            pltpu.VMEM((tokens, feat), BF16),
            pltpu.SemaphoreType.DMA((20,)),
            pltpu.SemaphoreType.DMA((20,)),
            pltpu.SemaphoreType.DMA((4,)),
        ]
    )
    results = pl.pallas_call(
        functools.partial(kernel, dp, tensors, tokens),
        out_shape=out_shape,
        in_specs=[vmem] * 7 + [anywhere],
        out_specs=[anywhere] * 3 + [vmem] * 3,
        scratch_shapes=scratch,
        compiler_params=pltpu.CompilerParams(
            collective_id=0, has_side_effects=True, vmem_limit_bytes=58 * 1024 * 1024
        ),
    )(
        query_raw,
        key_raw,
        value_rows,
        gain_query,
        gain_key,
        owner_id,
        utterance,
        cotangent,
    )
    return pl.pallas_call(
        copy_out,
        out_shape=out_shape,
        in_specs=[anywhere] * 6,
        out_specs=[anywhere] * 6,
        scratch_shapes=[pltpu.VMEM(out.shape, out.dtype) for out in out_shape]
        + [pltpu.SemaphoreType.DMA((6,)), pltpu.SemaphoreType.DMA((6,))],
        compiler_params=pltpu.CompilerParams(vmem_limit_bytes=58 * 1024 * 1024),
    )(*results)


def solution(mesh):
    wide = P("dp", "tensor")
    return jax.shard_map(
        shards,
        mesh=mesh,
        in_specs=(wide, wide, wide, P("tensor"), P("tensor"), P("dp"), P("dp"), wide),
        out_specs=(wide, wide, wide, wide, P("tensor"), P("tensor")),
        check_vma=False,
    )
```

```python
import functools
import math

import jax
import jax.numpy as jnp
from jax import lax
from jax.experimental import pallas as pl
from jax.experimental.pallas import tpu as pltpu
from jax.sharding import PartitionSpec as P

HD = 128
EPSILON = 1e-06
SLOT = 12
TILE = 16
HEADS = 6
GROUPS = 3
PART = 32
FAR = -(2.0**30)
F32 = jnp.float32
BF16 = jnp.bfloat16
MESH = pl.DeviceIdType.MESH
ORDER = {8: (3, -1, 2, -2, 0, -3, 1, 4), 4: (-1, 1, 0, 2)}
SHAPES = {64: (4, 8, 2), 16: (2, 4, 2)}


def mm(a, b):
    return lax.dot_general(a, b, (((1,), (0,)), ((), ())), preferred_element_type=F32)


def mm_nt(a, b):
    return lax.dot_general(a, b, (((1,), (1,)), ((), ())), preferred_element_type=F32)


def iota(shape, axis):
    return lax.broadcasted_iota(jnp.int32, shape, axis)


def ones_where(mask):
    return jnp.where(mask, 1.0, 0.0).astype(BF16)


def to_i32(x):
    return x.astype(jnp.int32)


def over(*parts):
    return jnp.concatenate(parts, axis=0)


def beside(*parts):
    return jnp.concatenate(parts, axis=1)


def kernel(
    dp,
    tensors,
    tokens,
    query_ref,
    key_ref,
    value_ref,
    gain_query_ref,
    gain_key_ref,
    owner_ref,
    utterance_ref,
    cotangent_hbm,
    attended_hbm,
    grad_query_hbm,
    grad_key_hbm,
    grad_value_ref,
    gain_query_out,
    gain_key_out,
    pack_first,
    pack_second,
    unpack_first,
    unpack_low,
    unpack_high_a,
    unpack_high_b,
    unpack_high_pair,
    normed,
    inverse_query_ref,
    inverse_key_ref,
    out_0,
    out_0_lent,
    out_1,
    out_1_lent,
    out_2,
    out_2_lent,
    out_3,
    out_3_lent,
    in_0,
    in_1,
    in_2,
    in_3,
    back_0,
    back_0_lent,
    back_1,
    back_1_lent,
    back_2,
    back_2_lent,
    back_3,
    back_3_lent,
    back_high,
    back_high_lent,
    back_high_got,
    home_0,
    home_1,
    home_2,
    home_3,
    value_own,
    grad_value_own,
    extend_query,
    extend_key,
    query_own,
    key_own,
    grad_query_own,
    grad_key_own,
    key_sum,
    value_sum,
    grad_qn,
    grad_kn,
    center_query_ref,
    center_key_ref,
    stat_norm,
    stat_center,
    gain_near,
    gain_far,
    cotangent_ref,
    attended_ref,
    grad_query_ref,
    grad_key_ref,
    send_sems,
    recv_sems,
    local_sems,
):
    size_y, size_z, size_c = SHAPES[dp]
    me = lax.axis_index("dp")
    my_x = lax.axis_index("tensor")
    my_c = me % size_c
    my_z = (me // size_c) % size_z
    my_y = me // (size_c * size_z)
    rows = dp * TILE
    own = dp * SLOT
    feat = HEADS * HD
    feat_total = feat * tensors
    blocks = dp // 16

    chips = size_y * size_z
    my_chip = my_y * size_z + my_z
    way = 1 - 2 * my_c
    z_of = {step: lax.rem(my_z + way * step + size_z, size_z) for step in ORDER[size_z]}
    y_of = [lax.rem(my_y + step, size_y) for step in range(size_y)]

    def put_to(source, target, send_index, recv_index, chip, core):
        pltpu.make_async_remote_copy(
            src_ref=source,
            dst_ref=target,
            send_sem=send_sems.at[send_index],
            recv_sem=recv_sems.at[recv_index],
            device_id={"dp": chip * size_c + core},
            device_id_type=MESH,
        ).start()

    def lend(outgoing, index):
        buffer, lent = outgoing
        put_to(lent, buffer.at[:, my_c], LENT + index, LENT + index, my_chip, 1 - my_c)

    def pair_of(target, chip):
        return target.at[pl.ds(chip * size_c, size_c)]

    def settle(outgoing, target, index):
        buffer, lent = outgoing
        pltpu.make_async_copy(lent, lent, recv_sems.at[LENT + index]).wait()
        pltpu.make_async_copy(
            buffer.at[my_chip], pair_of(target, my_chip), recv_sems.at[index]
        ).start()

    def send_part(outgoing, target, index, step):
        buffer, _ = outgoing
        landing = target.at[my_chip] if outgoing is back_3 else pair_of(target, my_chip)
        for place, step_z in enumerate(ORDER[size_z]):
            chip = lax.rem(my_y + step + place, size_y) * size_z + z_of[step_z]

            def send(chip=chip):
                put_to(buffer.at[chip], landing, index, index, chip, my_c)

            if step_z == 0:
                pl.when(step > 0)(send)
            else:
                send()

    def send_parts(outgoing, target, index, start, stop):
        def body(step, carry):
            send_part(outgoing, target, index, step)
            return carry

        lax.fori_loop(start, stop, body, 0)

    def scatter(outgoing, target, index):
        settle(outgoing, target, index)
        send_parts(outgoing, target, index, 0, size_y)

    def wait_recv(target, index):
        pltpu.make_async_copy(target, target, recv_sems.at[index]).wait()

    def wait_send(source, index, count):
        part = source.at[pl.ds(0, count)]
        pltpu.make_async_copy(part, part, send_sems.at[index]).wait()

    def share(buffer, slot, count, device_of, index):
        def step_body(step, carry):
            to = lax.rem(slot + step, count)
            pltpu.make_async_remote_copy(
                src_ref=buffer.at[slot],
                dst_ref=buffer.at[slot],
                send_sem=send_sems.at[index],
                recv_sem=recv_sems.at[index],
                device_id=device_of(to),
                device_id_type=MESH,
            ).start()
            return carry

        lax.fori_loop(1, count, step_body, 0)

    def share_wait(buffer, count, index):
        part = buffer.at[pl.ds(0, count - 1)]
        pltpu.make_async_copy(part, part, recv_sems.at[index]).wait()

    OUT, BACK, LENT, NORM, CENTER, NEAR, FARTHER, HIGH = 0, 4, 8, 16, 17, 18, 19, 20

    barrier = pltpu.get_barrier_semaphore()

    def greet(device_id):
        pl.semaphore_signal(barrier, inc=1, device_id=device_id, device_id_type=MESH)

    def greet_chip(step, carry):
        greet({"dp": lax.rem(me + step * size_c, dp)})
        return carry

    for step in range(1, tensors):
        greet({"tensor": lax.rem(my_x + step, tensors)})
    for step in range(size_y):
        greet({"dp": (y_of[step] * size_z + my_z) * size_c + 1 - my_c})
    lax.fori_loop(1, chips, greet_chip, 0)
    load_cotangent = pltpu.make_async_copy(cotangent_hbm, cotangent_ref, local_sems.at[0])
    load_cotangent.start()

    out_0, out_1, out_2, out_3 = zip(
        (out_0, out_1, out_2, out_3), (out_0_lent, out_1_lent, out_2_lent, out_3_lent)
    )
    back_3 = (back_3, back_3_lent)
    back_0, back_1, back_2 = zip(
        (back_0, back_1, back_2), (back_0_lent, back_1_lent, back_2_lent)
    )

    owner_row = owner_ref[...].reshape(1, tokens)
    chosen = jnp.where(iota((dp, tokens), 0) == owner_row, 1.0, 0.0)
    upper = ones_where(iota((tokens, tokens), 0) < iota((tokens, tokens), 1))
    rank_row = jnp.sum(mm(chosen.astype(BF16), upper) * chosen, axis=0, keepdims=True)
    code_row_f = owner_row.astype(F32) * TILE + rank_row

    def sent_place(peer):
        return lax.rem(peer + my_c, 2) * 8 + lax.div(lax.rem(peer, 16), 2)

    diagonal = iota((tokens, tokens), 0) == iota((tokens, tokens), 1)

    def as_column(row):
        return jnp.sum(jnp.where(diagonal, row, 0.0), axis=1, keepdims=True)

    rank_row = to_i32(rank_row)
    code_row = lax.div(owner_row, 16) * 256 + sent_place(owner_row) * TILE + rank_row
    none = -1

    utterance_col = to_i32(as_column(utterance_ref[...].reshape(1, tokens).astype(F32)))
    lane = iota((tokens, HD), 1)
    label_low = ones_where(lane == utterance_col)
    label_high = ones_where(lane == utterance_col + 64)

    def value_head(h):
        return value_ref[:, h * HD : (h + 1) * HD]

    def put(outgoing, block, lo, part):
        buffer, lent = outgoing
        width = part.shape[1]
        part = part.astype(BF16)
        out = pl.ds(block * 8, 8)
        buffer[out, my_c, :, lo : lo + width] = part[0:128].reshape(8, TILE, width)
        lent[out, :, lo : lo + width] = part[128:256].reshape(8, TILE, width)

    def pack_0(block, carry):
        span = pl.ds(pl.multiple_of(block * 256, 256), 256)
        row = iota((256, tokens), 0) + block * 256
        first = beside(
            ones_where(row == code_row),
            ones_where(row == jnp.where(rank_row < 4, code_row + 12, none)),
        )
        second = beside(
            ones_where(row == jnp.where(rank_row >= 4, code_row - 4, none)),
            ones_where(row == jnp.where(rank_row >= 4, code_row + 4, none)),
        )
        third = ones_where(row == jnp.where(rank_row < 8, code_row + 8, none))
        pack_first[span, :] = first
        pack_second[span, :] = second
        put(out_0, block, 0, mm(first, over(value_head(0), value_head(1))))
        put(out_0, block, HD, mm(second, over(value_head(1), label_high)) + mm(third, label_low))
        return carry

    lax.fori_loop(0, blocks, pack_0, 0)
    pl.semaphore_wait(barrier, chips - 1 + tensors - 1 + size_y)
    lend(out_0, OUT)

    half = iota((tokens, HD), 1) < 64
    query_f = query_ref[...].astype(F32)
    key_f = key_ref[...].astype(F32)
    stat_norm[my_x] = jnp.where(
        half,
        jnp.sum(query_f * query_f, axis=1, keepdims=True),
        jnp.sum(key_f * key_f, axis=1, keepdims=True),
    )
    share(stat_norm, my_x, tensors, lambda to: {"tensor": to}, NORM)
    scatter(out_0, in_0, OUT)


    code_col = to_i32(as_column(code_row_f))
    rank_col = code_col % TILE
    column = iota((tokens, rows), 1)
    unpack_first[...] = ones_where(column == code_col)
    unpack_low[...] = ones_where(column == jnp.where(rank_col < 4, code_col + 12, none))
    unpack_high_a[...] = ones_where(column == jnp.where(rank_col >= 4, code_col - 4, none))
    unpack_high_b[...] = ones_where(column == jnp.where(rank_col >= 4, code_col + 4, none))
    half_code = lax.div(code_col, 2) - lax.div(rank_col, 2) + rank_col - 4
    unpack_high_pair[...] = ones_where(
        iota((tokens, rows // 2), 1) == jnp.where(rank_col >= 4, half_code, none)
    )

    share_wait(stat_norm, tensors, NORM)
    total = stat_norm[0]
    for x in range(1, tensors):
        total = total + stat_norm[x]
    inverse = lax.rsqrt(total / feat_total + EPSILON)
    inverse_query_ref[...] = jnp.broadcast_to(inverse[:, 0:1], (tokens, HD))
    inverse_key_ref[...] = jnp.broadcast_to(inverse[:, 64:65], (tokens, HD))

    def gain_of(ref, h):
        return ref[h * HD : (h + 1) * HD].reshape(1, HD)

    def unit_query(h):
        return query_ref[:, h * HD : (h + 1) * HD].astype(F32) * inverse_query_ref[...]

    def unit_key(h):
        return key_ref[:, h * HD : (h + 1) * HD].astype(F32) * inverse_key_ref[...]

    def pack_qk(group, buffer, index):
        for h in (2 * group, 2 * group + 1):
            cols = slice(h * HD, (h + 1) * HD)
            normed[0:tokens, cols] = (gain_of(gain_query_ref, h) * unit_query(h)).astype(BF16)
            normed[tokens : 2 * tokens, cols] = (
                gain_of(gain_key_ref, h) * unit_key(h)
            ).astype(BF16)
        lo = group * 256

        def block_body(block, carry):
            span = pl.ds(pl.multiple_of(block * 256, 256), 256)
            first = pack_first[span, :]
            second = pack_second[span, :]
            keys = slice(tokens, 2 * tokens)
            put(buffer, block, 0, mm(first, normed[:, lo : lo + 256]))
            high = over(normed[keys, lo : lo + HD], normed[keys, lo + HD : lo + 256])
            put(buffer, block, 256, mm(second, high))
            if group == 1:
                v = [value_head(h) for h in range(HEADS)]
                put(buffer, block, 384, mm(first, over(beside(v[2], v[4]), beside(v[3], v[5]))))
                put(buffer, block, 640, mm(second, over(v[3], v[5])))
            return carry

        lax.fori_loop(0, blocks, block_body, 0)
        lend(buffer, index)

    pack_qk(0, out_1, OUT + 1)
    pack_qk(1, out_2, OUT + 2)
    scatter(out_1, in_1, OUT + 1)
    pack_qk(2, out_3, OUT + 3)
    settle(out_2, in_2, OUT + 2)
    send_part(out_2, in_2, OUT + 2, 0)

    def own_maps(own_axis, message_axis, shape, place_of):
        row = iota(shape, own_axis)
        message = iota(shape, message_axis)
        device = lax.div(row, SLOT)
        base = place_of(device) * TILE
        slot = row - device * SLOT
        first = ones_where(message == base + slot)
        low = ones_where((message == base + 12 + slot) & (slot < 4))
        high_a = ones_where((message == base + slot - 4) & (slot >= 4))
        high_b = ones_where((message == base + slot + 4) & (slot >= 4))
        labels = ones_where(message == base + 8 + slot - jnp.where(slot < 8, 0, 4))
        return first, low, high_a, high_b, labels

    first, low, high_a, high_b, label_map = own_maps(0, 1, (192, 256), lambda device: device)
    second_a = beside(low, high_a)
    second_b = beside(low, high_b)
    first_t, low_t, high_a_t, high_b_t, _ = own_maps(1, 0, (256, 192), sent_place)
    back_first = beside(first_t, low_t)
    back_second = beside(high_a_t, high_b_t)

    def message(buffer, src, tile):
        return buffer[src, :, tile * HD : (tile + 1) * HD].reshape(256, HD)

    wait_recv(in_0, OUT)

    def unpack_0(block, carry):
        span = pl.ds(pl.multiple_of(block * 192, 64), 192)
        src = pl.ds(block * 16, 16)
        t0 = message(in_0, src, 0)
        t1 = message(in_0, src, 1)
        value_own[0, span, :] = mm(first, t0).astype(BF16)
        value_own[1, span, :] = mm(second_a, over(t0, t1)).astype(BF16)
        found = mm(label_map, t1)
        early = iota((192, 1), 0) % SLOT < 8
        is_zero = jnp.where(early, found[:, 0:1], found[:, 64:65])
        is_one = jnp.where(early, found[:, 1:2], found[:, 65:66])
        spot = iota((192, HD), 1)
        member = jnp.where(
            spot == 0, is_zero, jnp.where(spot == 1, is_one, 1.0 - is_zero - is_one)
        )
        used = spot < 3
        extend_key[span, :] = jnp.where(used, member, 0.0).astype(BF16)
        extend_query[span, :] = jnp.where(used, FAR * (1.0 - member), 0.0).astype(BF16)
        return carry

    lax.fori_loop(0, blocks, unpack_0, 0)
    load_cotangent.wait()

    factor = HD**-0.5
    scale = factor * math.log2(math.e)
    chunk = 256 if own % 256 == 0 else own

    def softmax(scores):
        raised = jnp.exp2((scores - jnp.max(scores, axis=1, keepdims=True)) * scale)
        return (raised * (1.0 / jnp.sum(raised, axis=1, keepdims=True))).astype(BF16)

    def attention_group(group, send_in_chunk):
        buffer = (in_1, in_2, in_3)[group]
        wait_recv(buffer, OUT + 1 + group)

        def unpack_body(block, carry):
            span = pl.ds(pl.multiple_of(block * 192, 64), 192)
            src = pl.ds(block * 16, 16)
            t0, t1, t2 = (message(buffer, src, i) for i in range(3))
            q = mm(first, beside(t0, t1)).astype(BF16)
            query_own[0, span, :] = q[:, 0:HD]
            query_own[1, span, :] = q[:, HD : 2 * HD]
            key_own[0, span, :] = mm(second_a, over(t0, t2)).astype(BF16)
            key_own[1, span, :] = mm(second_b, over(t1, t2)).astype(BF16)
            if group == 1:
                t0, t1, t2 = (message(buffer, src, i) for i in range(3, 6))
                v = mm(first, beside(t0, t1)).astype(BF16)
                value_own[2, span, :] = v[:, 0:HD]
                value_own[4, span, :] = v[:, HD : 2 * HD]
                value_own[3, span, :] = mm(second_a, over(t0, t2)).astype(BF16)
                value_own[5, span, :] = mm(second_b, over(t1, t2)).astype(BF16)
            return carry

        lax.fori_loop(0, blocks, unpack_body, 0)
        key_sum[...] = jnp.zeros((2, HD, own), F32)
        value_sum[...] = jnp.zeros((2, HD, own), F32)

        def row_body(index, carry):
            send_in_chunk(index)
            span = pl.ds(pl.multiple_of(index * chunk, chunk), chunk)
            for local in range(2):
                head = 2 * group + local
                cols = slice(head * HD, (head + 1) * HD)
                keys = key_own[local]
                values = value_own[head]
                q = query_own[local, span, :]
                cot = cotangent_ref[span, cols]
                scores = mm_nt(beside(q, extend_query[span, :]), beside(keys, extend_key[...]))
                weights = over(*(softmax(scores[r : r + PART]) for r in range(0, chunk, PART)))
                attended = mm(weights, values).astype(BF16)
                attended_ref[span, cols] = attended
                delta = jnp.sum(cot.astype(F32) * attended.astype(F32), axis=1, keepdims=True)
                grad_weights = mm_nt(cot, values)
                grad_scores = over(
                    *(
                        (
                            weights[r : r + PART].astype(F32)
                            * (grad_weights[r : r + PART] - delta[r : r + PART])
                        ).astype(BF16)
                        for r in range(0, chunk, PART)
                    )
                )
                grad_query_own[local, span, :] = (mm(grad_scores, keys) * factor).astype(BF16)
                value_sum[local] += mm(cot.T, weights)
                key_sum[local] += mm(q.T, grad_scores)
            return carry

        lax.fori_loop(0, own // chunk, row_body, 0)
        for local in range(2):
            grad_key_own[local] = (key_sum[local].T * factor).astype(BF16)
            grad_value_own[2 * group + local] = value_sum[local].T.astype(BF16)

        target = (back_0, back_1, back_2)[group]

        def pack_body(block, carry):
            span = pl.ds(pl.multiple_of(block * 192, 64), 192)
            q = beside(grad_query_own[0, span, :], grad_query_own[1, span, :])
            k = [grad_key_own[i, span, :] for i in range(2)]
            put(target, block, 0, mm(back_first, over(q, beside(k[0], k[1]))))
            put(target, block, 256, mm(back_second, over(k[0], k[1])))
            if group == 1:
                v = [grad_value_own[i, span, :] for i in range(4)]
                put(
                    target, block, 384, mm(back_first, over(beside(v[0], v[2]), beside(v[1], v[3])))
                )
                put(target, block, 640, mm(back_second, over(v[1], v[3])))
            return carry

        lax.fori_loop(0, blocks, pack_body, 0)
        lend(target, BACK + group)

    def send_later(outgoing, target, index):
        chunks = own // chunk

        def in_chunk(position):
            start = 1 + position * (size_y - 1) // chunks
            stop = 1 + (position + 1) * (size_y - 1) // chunks
            send_parts(outgoing, target, index, start, stop)

        return in_chunk

    attention_group(0, send_later(out_2, in_2, OUT + 2))
    settle(out_3, in_3, OUT + 3)
    send_part(out_3, in_3, OUT + 3, 0)
    settle(back_0, home_0, BACK)
    send_part(back_0, home_0, BACK, 0)
    rest_out = send_later(out_3, in_3, OUT + 3)
    rest_back = send_later(back_0, home_0, BACK)

    def both_rests(position):
        rest_out(position)
        rest_back(position)

    attention_group(1, both_rests)
    settle(back_1, home_1, BACK + 1)
    send_part(back_1, home_1, BACK + 1, 0)
    attention_group(2, send_later(back_1, home_1, BACK + 1))

    high_t = jnp.where(my_c == 0, high_a_t, high_b_t)
    last, last_lent = back_3

    def pack_last(block, carry):
        span = pl.ds(pl.multiple_of(block * 192, 64), 192)
        out = pl.ds(block * 8, 8)
        v4 = grad_value_own[4, span, :]
        v5 = grad_value_own[5, span, :]
        part = mm(back_first, over(v4, v5)).astype(BF16)
        last[out, my_c] = part[0:128].reshape(8, TILE, HD)
        last_lent[out] = part[128:256].reshape(8, TILE, HD)
        part = mm(high_t, v5).astype(BF16)
        back_high[out] = part[0:128].reshape(8, TILE, HD)
        back_high_lent[out] = part[128:256].reshape(8, TILE, HD)
        return carry

    lax.fori_loop(0, blocks, pack_last, 0)
    lend(back_3, BACK + 3)
    put_to(back_high_lent, back_high_got, HIGH, HIGH, my_chip, 1 - my_c)
    scatter(back_2, home_2, BACK + 2)
    pltpu.make_async_copy(last_lent, last_lent, recv_sems.at[LENT + BACK + 3]).wait()
    pltpu.make_async_copy(back_high_got, back_high_got, recv_sems.at[HIGH]).wait()
    last[:, 2] = back_high[...] + back_high_got[...]
    pltpu.make_async_copy(
        last.at[my_chip], home_3.at[my_chip], recv_sems.at[BACK + 3]
    ).start()
    send_parts(back_3, home_3, BACK + 3, 0, size_y)
    save_attended = pltpu.make_async_copy(attended_ref, attended_hbm, local_sems.at[1])
    save_attended.start()

    near = my_y * size_c + my_c
    near_count = size_y * size_c
    center_query_ref[...] = jnp.zeros((tokens, HD), F32)
    center_key_ref[...] = jnp.zeros((tokens, HD), F32)
    gain_near[near] = jnp.zeros((16, HD), F32)

    def home_group(group):
        buffer = (home_0, home_1, home_2)[group]
        wait_recv(buffer, BACK + group)
        tile = lambda i: buffer[:, :, i * HD : (i + 1) * HD].reshape(rows, HD)
        both = beside(tile(0), tile(1))
        queries = mm(unpack_first[...], both)
        keys = mm(unpack_low[...], both)
        high = (mm(unpack_high_a[...], tile(2)), mm(unpack_high_b[...], tile(2)))
        for local in range(2):
            h = 2 * group + local
            cols = slice(h * HD, (h + 1) * HD)
            part = slice(local * HD, (local + 1) * HD)
            grad_q = queries[:, part].astype(BF16)
            grad_k = (keys[:, part] + high[local]).astype(BF16)
            grad_qn[:, cols] = grad_q
            grad_kn[:, cols] = grad_k
            term = grad_q.astype(F32) * unit_query(h)
            gain_near[near, h : h + 1, :] = jnp.sum(term, axis=0, keepdims=True)
            center_query_ref[...] += gain_of(gain_query_ref, h) * term
            term = grad_k.astype(F32) * unit_key(h)
            gain_near[near, 8 + h : 9 + h, :] = jnp.sum(term, axis=0, keepdims=True)
            center_key_ref[...] += gain_of(gain_key_ref, h) * term

    for group in range(3):
        home_group(group)

    stat_center[my_x] = jnp.where(
        half,
        jnp.sum(center_query_ref[...], axis=1, keepdims=True),
        jnp.sum(center_key_ref[...], axis=1, keepdims=True),
    )
    share(stat_center, my_x, tensors, lambda to: {"tensor": to}, CENTER)
    share(
        gain_near,
        near,
        near_count,
        lambda to: {"dp": ((to // size_c) * size_z + my_z) * size_c + to % size_c},
        NEAR,
    )

    def value_home(buffer, start, h):
        tile = lambda i: buffer[:, :, (start + i) * HD : (start + i + 1) * HD].reshape(rows, HD)
        both = beside(tile(0), tile(1))
        evens = mm(unpack_first[...], both)
        odds = mm(unpack_low[...], both)
        high = (mm(unpack_high_a[...], tile(2)), mm(unpack_high_b[...], tile(2)))
        for i in range(2):
            part = slice(i * HD, (i + 1) * HD)
            at = (h + 2 * i) * HD
            grad_value_ref[:, at : at + HD] = evens[:, part].astype(BF16)
            grad_value_ref[:, at + HD : at + 2 * HD] = (odds[:, part] + high[i]).astype(BF16)

    value_home(home_1, 3, 0)

    share_wait(gain_near, near_count, NEAR)
    total = gain_near[0]
    for i in range(1, near_count):
        total = total + gain_near[i]
    gain_far[my_z] = total
    share(
        gain_far,
        my_z,
        size_z,
        lambda to: {"dp": (my_y * size_z + to) * size_c + my_c},
        FARTHER,
    )

    share_wait(stat_center, tensors, CENTER)
    total = stat_center[0]
    for x in range(1, tensors):
        total = total + stat_center[x]
    total = total / feat_total
    center_q = jnp.broadcast_to(total[:, 0:1], (tokens, HD))
    center_k = jnp.broadcast_to(total[:, 64:65], (tokens, HD))
    for h in range(HEADS):
        cols = slice(h * HD, (h + 1) * HD)
        scaled = gain_of(gain_query_ref, h) * grad_qn[:, cols].astype(F32)
        grad_query_ref[:, cols] = (
            (scaled - unit_query(h) * center_q) * inverse_query_ref[...]
        ).astype(BF16)
        scaled = gain_of(gain_key_ref, h) * grad_kn[:, cols].astype(F32)
        grad_key_ref[:, cols] = (
            (scaled - unit_key(h) * center_k) * inverse_key_ref[...]
        ).astype(BF16)

    save_query = pltpu.make_async_copy(grad_query_ref, grad_query_hbm, local_sems.at[2])
    save_key = pltpu.make_async_copy(grad_key_ref, grad_key_hbm, local_sems.at[3])
    save_query.start()
    save_key.start()

    share_wait(gain_far, size_z, FARTHER)
    total = gain_far[0]
    for i in range(1, size_z):
        total = total + gain_far[i]
    for h in range(HEADS):
        gain_query_out[h * HD : (h + 1) * HD] = total[h : h + 1].reshape(HD)
        gain_key_out[h * HD : (h + 1) * HD] = total[8 + h : 9 + h].reshape(HD)

    wait_recv(home_3, BACK + 3)
    t0 = home_3[:, 0:2].reshape(rows, HD)
    t1 = home_3[:, 2].reshape(chips * TILE, HD)
    grad_value_ref[:, 4 * HD : 5 * HD] = mm(unpack_first[...], t0).astype(BF16)
    grad_value_ref[:, 5 * HD : 6 * HD] = (
        mm(unpack_low[...], t0) + mm(unpack_high_pair[...], t1)
    ).astype(BF16)

    save_attended.wait()
    save_query.wait()
    save_key.wait()
    outgoing = (out_0, out_1, out_2, out_3, back_0, back_1, back_2, back_3)
    for i, (buffer, lent) in enumerate(outgoing):
        wait_send(buffer, OUT + i, chips - 1)
        wait_send(lent, LENT + i, chips)
    wait_send(back_high_lent, HIGH, chips)
    wait_send(stat_norm, NORM, tensors - 1)
    wait_send(stat_center, CENTER, tensors - 1)
    wait_send(gain_near, NEAR, near_count - 1)
    wait_send(gain_far, FARTHER, size_z - 1)


def copy_out(*refs):
    count = (len(refs) - 2) // 3
    sources, targets, held = (refs[i * count : (i + 1) * count] for i in range(3))
    load_sems, save_sems = refs[-2:]
    loads, saves = [], []
    for i in range(count):
        extent = sources[i].shape[0]
        pieces = max(1, extent // 192) if len(sources[i].shape) == 2 else 1
        for piece in range(pieces):
            part = pl.ds(piece * (extent // pieces), extent // pieces)
            at = len(loads)
            loads.append(
                pltpu.make_async_copy(
                    sources[i].at[part], held[i].at[part], load_sems.at[at]
                )
            )
            saves.append(
                pltpu.make_async_copy(held[i].at[part], targets[i].at[part], save_sems.at[at])
            )
    for load in loads:
        load.start()
    for load, save in zip(loads, saves):
        load.wait()
        save.start()
    for save in saves:
        save.wait()


def shards(query_raw, key_raw, value_rows, gain_query, gain_key, owner_id, utterance, cotangent):
    dp = lax.axis_size("dp")
    tensors = lax.axis_size("tensor")
    tokens, feat = query_raw.shape
    rows = dp * TILE
    own = dp * SLOT
    _, size_z, _ = SHAPES[dp]
    vmem = pl.BlockSpec(memory_space=pltpu.VMEM)
    anywhere = pl.BlockSpec(memory_space=pl.ANY)
    out_shape = (
        jax.ShapeDtypeStruct((own, feat), BF16),
        jax.ShapeDtypeStruct((tokens, feat), BF16),
        jax.ShapeDtypeStruct((tokens, feat), BF16),
        jax.ShapeDtypeStruct((tokens, feat), BF16),
        jax.ShapeDtypeStruct((feat,), F32),
        jax.ShapeDtypeStruct((feat,), F32),
    )
    chips = dp // 2

    def outgoing(*widths):
        shapes = [
            shape for w in widths for shape in ((chips, 2, TILE, w), (chips, TILE, w))
        ]
        return [pltpu.VMEM(shape, BF16) for shape in shapes]

    def incoming(*widths):
        return [pltpu.VMEM((dp, TILE, width), BF16) for width in widths]

    scratch = (
        [
            pltpu.VMEM((rows, 2 * tokens), BF16),
            pltpu.VMEM((rows, 2 * tokens), BF16),
            pltpu.VMEM((tokens, rows), BF16),
            pltpu.VMEM((tokens, rows), BF16),
            pltpu.VMEM((tokens, rows), BF16),
            pltpu.VMEM((tokens, rows), BF16),
            pltpu.VMEM((tokens, rows // 2), BF16),
            pltpu.VMEM((2 * tokens, feat), BF16),
            pltpu.VMEM((tokens, HD), F32),
            pltpu.VMEM((tokens, HD), F32),
        ]
        + outgoing(256, 384, 768, 384)
        + incoming(256, 384, 768, 384)
        + outgoing(384, 768, 384)
        + [pltpu.VMEM((chips, 3, TILE, HD), BF16)]
        + [pltpu.VMEM((chips, TILE, HD), BF16) for _ in range(4)]
        + incoming(384, 768, 384)
        + [pltpu.VMEM((chips, 3, TILE, HD), BF16)]
        + [
            pltpu.VMEM((HEADS, own, HD), BF16),
            pltpu.VMEM((HEADS, own, HD), BF16),
            pltpu.VMEM((own, HD), BF16),
            pltpu.VMEM((own, HD), BF16),
            pltpu.VMEM((2, own, HD), BF16),
            pltpu.VMEM((2, own, HD), BF16),
            pltpu.VMEM((2, own, HD), BF16),
            pltpu.VMEM((2, own, HD), BF16),
            pltpu.VMEM((2, HD, own), F32),
            pltpu.VMEM((2, HD, own), F32),
            pltpu.VMEM((tokens, feat), BF16),
            pltpu.VMEM((tokens, feat), BF16),
            pltpu.VMEM((tokens, HD), F32),
            pltpu.VMEM((tokens, HD), F32),
            pltpu.VMEM((tensors, tokens, HD), F32),
            pltpu.VMEM((tensors, tokens, HD), F32),
            pltpu.VMEM((dp // size_z, 16, HD), F32),
            pltpu.VMEM((size_z, 16, HD), F32),
            pltpu.VMEM((own, feat), BF16),
            pltpu.VMEM((own, feat), BF16),
            pltpu.VMEM((tokens, feat), BF16),
            pltpu.VMEM((tokens, feat), BF16),
            pltpu.SemaphoreType.DMA((21,)),
            pltpu.SemaphoreType.DMA((21,)),
            pltpu.SemaphoreType.DMA((4,)),
        ]
    )
    results = pl.pallas_call(
        functools.partial(kernel, dp, tensors, tokens),
        out_shape=out_shape,
        in_specs=[vmem] * 7 + [anywhere],
        out_specs=[anywhere] * 3 + [vmem] * 3,
        scratch_shapes=scratch,
        compiler_params=pltpu.CompilerParams(
            collective_id=0, has_side_effects=True, vmem_limit_bytes=58 * 1024 * 1024
        ),
    )(
        query_raw,
        key_raw,
        value_rows,
        gain_query,
        gain_key,
        owner_id,
        utterance,
        cotangent,
    )
    return pl.pallas_call(
        copy_out,
        out_shape=out_shape,
        in_specs=[anywhere] * 6,
        out_specs=[anywhere] * 6,
        scratch_shapes=[pltpu.VMEM(out.shape, out.dtype) for out in out_shape]
        + [pltpu.SemaphoreType.DMA((16,)), pltpu.SemaphoreType.DMA((16,))],
        compiler_params=pltpu.CompilerParams(vmem_limit_bytes=58 * 1024 * 1024),
    )(*results)


def solution(mesh):
    wide = P("dp", "tensor")
    return jax.shard_map(
        shards,
        mesh=mesh,
        in_specs=(wide, wide, wide, P("tensor"), P("tensor"), P("dp"), P("dp"), wide),
        out_specs=(wide, wide, wide, wide, P("tensor"), P("tensor")),
        check_vma=False,
    )
```
